32 devices in a mesh: dp: 4 (over y, x), seq: 8 (over z, core).
Axes of the slice: x: 2, y: 2, z: 4, core: 2. Of those that a mesh axis runs over, the one named last changes fastest.
Arguments:
- tokens: bfloat16 [2, 4, 1024, 768], P(None, 'dp', 'seq'), may hold values from -6 to 6
- cotangent: bfloat16 [2, 4, 1024, 768], P(None, 'dp', 'seq'), may hold values from -6 to 6
- expert_ids: int32 [2, 4, 1024, 2], P(None, 'dp', 'seq'), may hold values from 0 to 15, all different within a row; in each aligned block of 128 rows (0 to 127, 128 to 255, ..., all dimensions but the last counted through in order) at most 18 rows name the same one
- buckets: int32 [1024], replicated, may hold values from 0 to 31
- gain_attn: bfloat16 [768], P(('dp', 'seq')), may hold values from 0.5 to 1.5
- w_qkv: bfloat16 [768, 2304], P(('dp', 'seq')), may hold values from -0.21875 to 0.21875
- rel_bias: bfloat16 [32, 12], replicated, may hold values from -4 to 4
- w_attn_out: bfloat16 [768, 768], P(('dp', 'seq')), may hold values from -2 to 2
- gain_moe: bfloat16 [768], P(('dp', 'seq')), may hold values from 0.5 to 1.5
- router: bfloat16 [768, 16], P(('dp', 'seq')), may hold values from -0.15625 to 0.15625
- w_up: bfloat16 [16, 768, 3072], P('seq', None, 'dp'), may hold values from -0.21875 to 0.21875
- w_down: bfloat16 [16, 768, 3072], P('seq', None, 'dp'), may hold values from -0.109375 to 0.109375
Outputs:
- mixed_out: bfloat16 [2, 4, 1024, 768], P(None, 'dp', 'seq')
- grad_tokens: bfloat16 [2, 4, 1024, 768], P(None, 'dp', 'seq')
- grad_gain_attn: float32 [768], P(('dp', 'seq'))
- grad_qkv: float32 [768, 2304], P(('dp', 'seq'))
- grad_rel_bias: float32 [32, 12], replicated
- grad_attn_out: float32 [768, 768], P(('dp', 'seq'))
- grad_gain_moe: float32 [768], P(('dp', 'seq'))
- grad_router: float32 [768, 16], P(('dp', 'seq'))
- grad_up: float32 [16, 768, 3072], P('seq', None, 'dp')
- grad_down: float32 [16, 768, 3072], P('seq', None, 'dp')
The draws below stay inside these ranges and needn't reach their ends.
Inputs may be any that keep to these rules, and one draw needn't show every extreme that they name: `expert_ids`: the two ids of a token differ. In each aligned block of 128 positions of one sequence (the positions of one device), no expert is chosen more than 18 times, and in some blocks one expert is chosen exactly 18 times; every expert is chosen somewhere.
All inputs are finite; a program needn't handle non-finite values.
Results may differ from the reference program's by a relative error of at most 0.02.
Values may be sent and summed in bfloat16 or wider, within the bound.
No kernel may reach another device: no remote copies, remote signals or barrier semaphores. Data moves between devices by JAX's collectives and lax.ppermute only.
A program may use at most 192 MiB of HBM per device.

```python
import math
import jax
import jax.numpy as jnp
import numpy as np
from jax import lax

D = 768
HEADS = 12
HD = 64
FF = 3072
NBUCKETS = 32
TOPK = 2
SEQ_TOK = 128
MICRO = 2
EXPERTS = 16
LENGTH = 1024
SEQS = 4
CAP = 18


def touch_ends(values, stream_key, low, high):
    spot = [jax.random.randint(jax.random.fold_in(stream_key, axis), (), 0, length) for axis, length in enumerate(values.shape)]
    longest = values.shape.index(max(values.shape))
    neighbour = spot[:longest] + [(spot[longest] + 1) % values.shape[longest]] + spot[longest + 1:]
    return values.at[tuple(spot)].set(low).at[tuple(neighbour)].set(high)


def block_levels(rng, shape, split, least, high):
    level, own = 1.0, jax.random.fold_in(rng, 6)
    for dim, parts in split:
        heights = jnp.exp(jax.random.uniform(jax.random.fold_in(own, dim), (parts,), jnp.float32, least / len(split), high / len(split)))
        level = level * jnp.repeat(heights, shape[dim] // parts).reshape([-1 if axis == dim else 1 for axis in range(len(shape))])
    return level


def shared_out(stream_key, own, number, rows, number_of, top, limit, lean):
    order = jax.random.permutation(stream_key, number_of)
    heavy_load, ordinary = load_shares(number_of, rows * top, limit, lean, True), load_shares(number_of, rows * top, limit, lean, False)
    places = jnp.arange(number_of)

    def named(tallies, turn):
        used = int((tallies > 0).sum())
        fixed = max(1, used // 4)
        passed = fixed + (places - fixed + turn * (used - fixed)) % max(1, number_of - fixed)
        return jnp.zeros((number_of,), jnp.int32).at[order[jnp.where(places < fixed, places, passed)]].set(jnp.asarray(tallies, jnp.int32))

    tallies = jnp.where(number % 4 == 0, named(heavy_load, number // 4), named(ordinary, number - number // 4 - 1))
    mixed = jax.random.permutation(jax.random.fold_in(own, 3), number_of)
    donor, receiver = mixed[0:number_of // 2 * 2:2], mixed[1:number_of // 2 * 2:2]
    slack = jnp.minimum(tallies[donor] - 1, limit - tallies[receiver]) // 2
    slack = jnp.where((donor == order[0]) | (receiver == order[0]) | (tallies[receiver] == 0), 0, jnp.maximum(slack, 0))
    passed = jax.random.randint(jax.random.fold_in(own, 4), (number_of // 2,), 0, 1 << 20) % (slack + 1)
    tallies = tallies.at[donor].add(-passed).at[receiver].add(passed)
    labels = jnp.searchsorted(jnp.cumsum(tallies), jnp.arange(rows * top), side="right").astype(jnp.int32)
    grid = labels.reshape(top, rows).T
    grid = grid[jax.random.permutation(jax.random.fold_in(own, 1), rows)]
    turn = jax.random.randint(jax.random.fold_in(own, 2), (rows, 1), 0, top)
    return jnp.take_along_axis(grid, (jnp.arange(top)[None, :] + turn) % top, axis=1)


def load_shares(number_of, total, reach, skew, full):
    loads = [(1 << 20) // math.isqrt(grade ** skew) + 1 for grade in range(1, number_of + 1)]
    largest = reach if full else min(reach, max(-(-total // number_of), total * loads[0] // sum(loads)))
    least = 1 if total - largest >= number_of - 1 else 0
    given, surplus = [largest] + [least] * (number_of - 1), total - largest - least * (number_of - 1)
    while surplus > 0:
        movable = [i for i in range(1, number_of) if given[i] < largest] or [i for i in range(1, number_of) if given[i] < reach]
        pool, left = sum([loads[i] for i in movable]), surplus
        for i in movable:
            addition = min(reach - given[i], max(1, left * loads[i] // pool), surplus)
            given[i] = given[i] + addition
            surplus = surplus - addition
    return np.array(given)


def normal_values(rng, dims, scale, limit, split=(), kind=jnp.bfloat16):
    values = jax.random.normal(rng, dims, jnp.float32) * scale
    if len(split) > 0:
        values = block_levels(rng, dims, split, -0.22, 0.18) * values
    return jnp.clip(values, min=-limit, max=limit).astype(kind)


def setup_inputs(seed: int = 0) -> dict:
    arg_keys = jax.random.split(jax.random.key(seed), 13)
    tokens = normal_values(arg_keys[0], (MICRO, SEQS, LENGTH, D), 1.0, 6.0, ((1, 4), (2, 8)))
    cotangent = normal_values(arg_keys[1], (MICRO, SEQS, LENGTH, D), 1.0, 6.0, ((1, 4), (2, 8)))
    expert_ids_keys = jax.random.split(jax.random.fold_in(arg_keys[2], 1), MICRO * SEQS * LENGTH // SEQ_TOK)
    expert_ids_turns = jax.random.permutation(jax.random.fold_in(arg_keys[2], 3), MICRO * SEQS * LENGTH // SEQ_TOK)
    expert_ids = jax.vmap(lambda own, number: shared_out(jax.random.fold_in(arg_keys[2], 2), own, number, SEQ_TOK, EXPERTS, TOPK, CAP, 1))(expert_ids_keys, expert_ids_turns).reshape((MICRO, SEQS, LENGTH, TOPK))
    buckets = touch_ends(jax.random.randint(arg_keys[3], (LENGTH,), 0, NBUCKETS), jax.random.fold_in(arg_keys[3], 1), 0, NBUCKETS - 1).astype(jnp.int32)
    gain_attn = jnp.clip(1.0 + 0.1 * jax.random.normal(arg_keys[4], (D,), jnp.float32), 0.5, 1.5).astype(jnp.bfloat16)
    w_qkv = normal_values(arg_keys[5], (D, 3 * D), D ** -0.5, 0.21875, ((0, 32),))
    rel_bias = normal_values(arg_keys[6], (NBUCKETS, HEADS), 1.0, 4.0)
    w_attn_out = normal_values(arg_keys[7], (D, D), (D // 96) ** -0.5, 2.0, ((0, 32),))
    gain_moe = jnp.clip(1.0 + 0.1 * jax.random.normal(arg_keys[8], (D,), jnp.float32), 0.5, 1.5).astype(jnp.bfloat16)
    router = normal_values(arg_keys[9], (D, EXPERTS), (2 * D) ** -0.5, 0.15625, ((0, 32),))
    w_up = normal_values(arg_keys[10], (EXPERTS, D, FF), D ** -0.5, 0.21875, ((0, 8), (2, 4)))
    w_down = normal_values(arg_keys[11], (EXPERTS, D, FF), FF ** -0.5, 0.109375, ((0, 8), (2, 4)))
    return dict(tokens=tokens, cotangent=cotangent, expert_ids=expert_ids, buckets=buckets, gain_attn=gain_attn, w_qkv=w_qkv, rel_bias=rel_bias, w_attn_out=w_attn_out, gain_moe=gain_moe, router=router, w_up=w_up, w_down=w_down)


@jax.custom_vjp
def low(v):
    return lax.optimization_barrier(v.astype(jnp.bfloat16)).astype(jnp.float32)

@jax.custom_vjp
def low_back(v):
    return v

def low_keep(v):
    return (low(v), None)

def low_pass(kept, grad):
    return (grad,)

def back_keep(v):
    return (v, None)

def back_low(kept, grad):
    return (low(grad),)
low.defvjp(low_keep, low_pass)
low_back.defvjp(back_keep, back_low)
eps_norm = 1e-06
neg_big = -1e+30
highest = lax.Precision.HIGHEST

def rms_scale(values, gain):
    return values * lax.rsqrt(lax.optimization_barrier(jnp.mean(values * values, axis=-1, keepdims=True)) + eps_norm) * gain

def attend_one(query, keys, values, table, buckets):
    length = query.shape[0]
    block_rows = math.gcd(length, 512)
    key_pos = jnp.arange(length, dtype=jnp.int32)
    qk_scale = 1.0 / math.sqrt(HD)

    def one_block(block_index):
        start = (block_index * block_rows).astype(jnp.int32)
        query_blk = lax.dynamic_slice_in_dim(query, start, block_rows, 0)
        query_pos = start + jnp.arange(block_rows, dtype=jnp.int32)
        distance = query_pos[:, None] - key_pos[None, :]
        visible = distance >= 0
        bucket_ids = buckets[jnp.clip(distance, 0, length - 1).astype(jnp.int32)]
        pos_bias = jnp.transpose(table[bucket_ids], (2, 0, 1))
        scores = jnp.einsum('qhd,khd->hqk', query_blk, keys, precision=highest) * qk_scale + pos_bias
        scores = low_back(scores)
        scores = jnp.where(visible[None], scores, neg_big)
        attn_prob = jax.nn.softmax(scores, axis=-1)
        return jnp.einsum('hqk,khd->qhd', low(attn_prob), values, precision=highest)
    blocks = lax.map(jax.checkpoint(one_block), jnp.arange(length // block_rows, dtype=jnp.int32))
    return blocks.reshape(length, query.shape[1], query.shape[2])

def expert_slots(normed, picked_ids, weight_up, weight_down):
    total_rows = normed.shape[0]
    pieces = total_rows // SEQ_TOK
    slot_ids = picked_ids.reshape(pieces, TOPK * SEQ_TOK)
    expert_hot = (slot_ids[..., None] == jnp.arange(EXPERTS, dtype=jnp.int32)).astype(jnp.int32)
    slot_rank = lax.optimization_barrier(jnp.sum(expert_hot * (jnp.cumsum(expert_hot, axis=1) - 1), axis=-1))
    piece_index = jnp.arange(pieces, dtype=jnp.int32)[:, None]
    slot_dest = (slot_ids * (pieces * CAP) + piece_index * CAP + slot_rank).reshape(-1).astype(jnp.int32)
    copies = low_back(jnp.repeat(normed, TOPK, axis=0))
    buffer = jnp.zeros((EXPERTS * pieces * CAP, D), jnp.float32).at[slot_dest].add(copies)
    buffer = buffer.reshape(EXPERTS, pieces * CAP, D)
    pre_act = low_back(jnp.einsum('erd,edf->erf', buffer, weight_up, precision=highest))
    hidden = low(jax.nn.gelu(pre_act, approximate=False))
    expert_out = low_back(low(jnp.einsum('erf,edf->erd', hidden, weight_down, precision=highest)))
    return expert_out.reshape(EXPERTS * pieces * CAP, D)[slot_dest].reshape(total_rows, TOPK, D)

def group_forward(group_in, group_ids, buckets, params):
    gain_first, weight_qkv, table, weight_out, gain_second, weight_router, weight_up, weight_down = params
    group_size = group_in.shape[0]
    total_rows = group_size * LENGTH
    resid_in = group_in.reshape(total_rows, D)
    normed_first = low(rms_scale(resid_in, gain_first))
    qkv_rows = jnp.dot(normed_first, weight_qkv, precision=highest)
    query = low_back(low(qkv_rows[:, :D])).reshape(group_size, LENGTH, HEADS, HD)
    keys = low_back(low(qkv_rows[:, D:2 * D])).reshape(group_size, LENGTH, HEADS, HD)
    values = low_back(low(qkv_rows[:, 2 * D:])).reshape(group_size, LENGTH, HEADS, HD)
    attended = jax.vmap(lambda qa, ka, va: attend_one(qa, ka, va, table, buckets))(query, keys, values)
    attended = low_back(low(attended.reshape(total_rows, D)))
    resid_mid = resid_in + low_back(jnp.dot(attended, weight_out, precision=highest))
    normed_second = low(rms_scale(resid_mid, gain_second))
    logits = jnp.dot(normed_second, weight_router, precision=highest)
    probs = jax.nn.softmax(logits, axis=-1)
    picked_ids = group_ids.reshape(total_rows, TOPK)
    picked = jnp.take_along_axis(probs, picked_ids, axis=1)
    gates = picked / lax.optimization_barrier(jnp.sum(picked, axis=1, keepdims=True))
    slot_out = expert_slots(normed_second, picked_ids, weight_up, weight_down)
    mixed = resid_mid + lax.optimization_barrier(jnp.sum(gates[..., None] * slot_out, axis=1))
    return mixed.reshape(group_in.shape)

def reference(tokens, cotangent, expert_ids, buckets, gain_attn, w_qkv, rel_bias, w_attn_out, gain_moe, router, w_up, w_down):
    group_size = math.gcd(MICRO * SEQS, max(1, 4096 // LENGTH))
    ids_shaped = expert_ids.reshape(-1, group_size, LENGTH, TOPK)

    def forward(inputs, gain_first, weight_qkv, table, weight_out, gain_second, weight_router, weight_up, weight_down):
        params = (gain_first, weight_qkv, table, weight_out, gain_second, weight_router, weight_up, weight_down)
        shaped = inputs.reshape(-1, group_size, LENGTH, D)
        mixed = lax.map(lambda pair: group_forward(pair[0], pair[1], buckets, params), (shaped, ids_shaped))
        return mixed.reshape(inputs.shape)
    floats = (tokens, gain_attn, w_qkv, rel_bias, w_attn_out, gain_moe, router, w_up, w_down)
    floats = tuple((item.astype(jnp.float32) for item in floats))
    mixed, pullback = jax.vjp(forward, *floats)
    grads = pullback(cotangent.astype(jnp.float32))
    return (mixed.astype(jnp.bfloat16), grads[0].astype(jnp.bfloat16), grads[1], grads[2], grads[3], grads[4], grads[5], grads[6], grads[7], grads[8])
```

```python
import functools
import math

import jax
import jax.numpy as jnp
from jax import lax
from jax.experimental import pallas as pl
from jax.experimental.pallas import tpu as pltpu
from jax.sharding import PartitionSpec as P

HD = 64
LANES = 128
EPS = 1e-06
NEG = -1e30
F32 = jnp.float32
BF16 = jnp.bfloat16
VMEM_BYTES = 56 * 1024 * 1024
INV_SQRT2 = 1.0 / math.sqrt(2.0)
INV_SQRT2PI = 1.0 / math.sqrt(2.0 * math.pi)


def mm(a, b):
    return lax.dot_general(a, b, (((1,), (0,)), ((), ())), preferred_element_type=F32)


def mm_nt(a, b):
    return lax.dot_general(a, b, (((1,), (1,)), ((), ())), preferred_element_type=F32)


def mm_tn(a, b):
    return lax.dot_general(a, b, (((0,), (0,)), ((), ())), preferred_element_type=F32)


def iota(shape, dim):
    return lax.broadcasted_iota(jnp.int32, shape, dim)


def split3(v):
    hi = v.astype(BF16).astype(F32)
    rest = v - hi
    mid = rest.astype(BF16).astype(F32)
    return hi, mid, rest - mid


def call(kernel, outs, ins, scratch=(), smem=0, name=None):
    spec = [pl.BlockSpec(memory_space=pltpu.SMEM)] * smem
    spec += [pl.BlockSpec(memory_space=pltpu.VMEM)] * (len(ins) - smem)
    return pl.pallas_call(
        kernel,
        out_shape=[jax.ShapeDtypeStruct(s, d) for s, d in outs],
        in_specs=spec,
        out_specs=[pl.BlockSpec(memory_space=pltpu.VMEM)] * len(outs),
        scratch_shapes=list(scratch),
        compiler_params=pltpu.CompilerParams(vmem_limit_bytes=VMEM_BYTES),
        name=name,
    )(*ins)


def route_kernel(dims, ids_ref, cot_ref, slot_ref, *out_refs):
    rows, experts, local, seq, cp = dims
    ids = ids_ref[...]
    expert = iota((rows, experts), 1)
    hot = [(ids[:, j : j + 1] == expert).astype(F32) for j in range(2)]
    before = (iota((rows, rows), 0) > iota((rows, rows), 1)).astype(BF16)
    rank = mm(before, (hot[0] + hot[1]).astype(BF16))
    cols = []
    for j in range(2):
        own = jnp.sum(hot[j] * rank, axis=1, keepdims=True).astype(jnp.int32)
        e = ids[:, j : j + 1]
        cols.append((e % local) * (seq * cp) + (e // local) * cp + own)
    lane = iota((rows, LANES), 1)
    slot_ref[...] = jnp.where(lane == 0, cols[0], cols[1])
    cot = cot_ref[...]
    for e, out_ref in enumerate(out_refs):
        place = place_both(cols, e, seq * cp)
        out_ref[...] = mm_tn(place, cot).astype(BF16)


def place_one(col, e, count):
    return (iota((col.shape[0], count), 1) + e * count == col).astype(BF16)


def place_both(cols, e, count):
    where = iota((cols[0].shape[0], count), 1) + e * count
    return jnp.logical_or(where == cols[0], where == cols[1]).astype(BF16)


def attn_fwd_kernel(dims, meta_ref, *refs):
    half, dp, hpd, block, gain_lane, scale = dims
    own, sib, wp = refs[:half], refs[half : 2 * half], refs[2 * half : 2 * half + dp]
    brev_ref = refs[2 * half + dp]
    o_ref, qkv_ref, xn_ref, w_ref, lse_ref, slab_ref, gain_ref = refs[2 * half + dp + 1 :]
    z, c, d = meta_ref[0], meta_ref[1], meta_ref[2]
    part = wp[0].shape[0]
    for j in range(dp):
        w_ref[pl.ds(pl.multiple_of((d ^ j) * part, part), part), :] = wp[j][...]
    width_c = w_ref.shape[1]
    turned = jnp.transpose(w_ref[:, width_c - LANES :].astype(F32))
    gain = turned[gain_lane : gain_lane + 1, :]
    gain_ref[...] = gain
    rows = own[0].shape[0]
    for group, core in ((own, c), (sib, 1 - c)):
        for k in range(half):
            x = group[k][...].astype(F32)
            r = lax.rsqrt(jnp.mean(x * x, axis=1, keepdims=True) + EPS)
            start = pl.multiple_of((2 * (z ^ k) + core) * rows, rows)
            xn_ref[pl.ds(start, rows), :] = (x * r * gain).astype(BF16)
    length = xn_ref.shape[0]
    for i in range(length // block):
        part_rows = slice(i * block, (i + 1) * block)
        qkv_ref[part_rows, :] = mm(xn_ref[part_rows, :], w_ref[...]).astype(BF16)
    span = length + block
    width_h = hpd * HD
    for h in range(hpd):
        base = brev_ref[h : h + 1, :]
        rolled = [base if i == 7 else pltpu.roll(base, span - (7 - i), 1) for i in range(8)]
        slab = jnp.concatenate(rolled, axis=0)
        n = 8
        while n < block:
            slab = jnp.concatenate([pltpu.roll(slab, span - n, 1), slab], axis=0)
            n *= 2
        slab_ref[h] = slab[:, :length]
    lane = iota((block, LANES), 1)
    for i in range(length // block):
        q_rows = slice(i * block, (i + 1) * block)
        keys = (i + 1) * block
        lse = jnp.zeros((block, LANES), F32)
        for h in range(hpd):
            q = qkv_ref[q_rows, h * HD : (h + 1) * HD] * jnp.asarray(scale, BF16)
            k = qkv_ref[:keys, width_h + h * HD : width_h + (h + 1) * HD]
            v = qkv_ref[:keys, 2 * width_h + h * HD : 2 * width_h + (h + 1) * HD]
            s = mm_nt(q, k) + slab_ref[h, :, length - keys :]
            top = jnp.max(s, axis=1, keepdims=True)
            e = jnp.exp(s - top)
            total = jnp.sum(e, axis=1, keepdims=True)
            p = (e * (1.0 / total)).astype(BF16)
            o_ref[q_rows, h * HD : (h + 1) * HD] = mm(p, v).astype(BF16)
            lse = jnp.where(lane == h, top + jnp.log(total), lse)
        lse_ref[q_rows, :] = lse


def attn_bwd_kernel(dims, meta_ref, do_ref, qkv_ref, xn_ref, w_ref, lse_ref, slab_ref, *refs):
    half, hpd, block, scale = dims
    dx_own, dx_sib, gq_ref, gb_ref, dqkv_ref, dk_ref, dv_ref, db_ref = refs
    z, c = meta_ref[0], meta_ref[1]
    length = qkv_ref.shape[0]
    width_h = hpd * HD
    blocks = length // block
    dqkv_ref[...] = jnp.zeros_like(dqkv_ref)
    for h in range(hpd):
        cols = slice(h * HD, (h + 1) * HD)
        k_cols = slice(width_h + h * HD, width_h + (h + 1) * HD)
        v_cols = slice(2 * width_h + h * HD, 2 * width_h + (h + 1) * HD)
        for i in range(blocks - 1, -1, -1):
            rows = slice(i * block, (i + 1) * block)
            keys = (i + 1) * block
            q = qkv_ref[rows, cols] * jnp.asarray(scale, BF16)
            k = qkv_ref[:keys, k_cols]
            v = qkv_ref[:keys, v_cols]
            do = do_ref[rows, cols]
            s = mm_nt(q, k) + slab_ref[h, :, length - keys :]
            p = jnp.exp(s - lse_ref[rows, h : h + 1])
            dp = mm_nt(do, v)
            delta = jnp.sum(p * dp, axis=1, keepdims=True)
            ds32 = p * (dp - delta)
            ds = ds32.astype(BF16)
            dqkv_ref[rows, cols] = (mm(ds, k) * scale).astype(BF16)
            dk = mm_tn(ds, q)
            dv = mm_tn(p.astype(BF16), do)
            if i == blocks - 1:
                dk_ref[...] = dk
                dv_ref[...] = dv
                db_ref[:, :length] = ds.astype(F32)
            else:
                dk_ref[:keys, :] += dk
                dv_ref[:keys, :] += dv
                db_ref[:, length - keys : length] += ds.astype(F32)
        dqkv_ref[:, k_cols] = dk_ref[...].astype(BF16)
        dqkv_ref[:, v_cols] = dv_ref[...].astype(BF16)
        db_ref[:, length:] = jnp.zeros((block, block), F32)
        n = block
        acc = db_ref[...]
        while n > 1:
            n //= 2
            acc = pltpu.roll(acc[:n], n, 1) + acc[n:]
        gb_ref[h : h + 1, :] = acc
    rows = dx_own.shape[1]
    w = w_ref[...]
    for out_ref, core in ((dx_own, c), (dx_sib, 1 - c)):
        for k in range(half):
            start = pl.multiple_of((2 * (z ^ k) + core) * rows, rows)
            out_ref[k] = mm_nt(dqkv_ref[pl.ds(start, rows), :], w).astype(BF16)
    gq_ref[...] = mm_tn(xn_ref[...], dqkv_ref[...]).astype(BF16)


def pick_probs(ids, probs):
    expert = iota(probs.shape, 1)
    hot = [(ids[:, j : j + 1] == expert).astype(F32) for j in range(2)]
    picked = [jnp.sum(probs * one, axis=1, keepdims=True) for one in hot]
    total = picked[0] + picked[1]
    return hot, total, [one / total for one in picked]


def norm_parts(x1):
    r = lax.rsqrt(jnp.mean(x1 * x1, axis=1, keepdims=True) + EPS)
    return r, x1 * r


def mid_kernel(dims, o_ref, x_ref, wo_ref, router_ref, gain_ref, ids_ref, slot_ref, *refs):
    seqs, groups, cp, dead, per_expert = dims
    x1_ref, xn_ref, prob_ref, *send_refs = refs
    rows = x_ref.shape[0] // seqs
    width_h = o_ref.shape[2]
    for m in range(seqs):
        part = slice(m * rows, (m + 1) * rows)
        acc = x_ref[part, :].astype(F32)
        for g in range(groups):
            acc += mm(o_ref[m * groups + g], wo_ref[g * width_h : (g + 1) * width_h, :])
        x1_ref[part, :] = acc
    r, u = norm_parts(x1_ref[...])
    xn = (u * gain_ref[...].astype(F32)).astype(BF16)
    xn_ref[...] = xn
    logits = mm(xn, router_ref[...])
    e = jnp.exp(logits - jnp.max(logits, axis=1, keepdims=True))
    probs = e / jnp.sum(e, axis=1, keepdims=True)
    prob_ref[...] = probs
    ids = ids_ref[...]
    _, _, gates = pick_probs(ids, probs)
    cols = [slot_ref[:, j : j + 1] for j in range(2)]
    lane = iota((xn.shape[0], LANES), 1)
    carried, bases = [], []
    for j in range(2):
        rank = cols[j] % cp
        bases.append(cols[j] - rank + dead)
        hi, mid, low = split3(gates[j])
        value = jnp.where(lane < cp, hi, jnp.where(lane < 2 * cp, mid, low))
        keep = jnp.logical_and(lane % cp == rank, lane < 3 * cp)
        carried.append(jnp.where(keep, value, 0.0).astype(BF16))
    for k, send_ref in enumerate(send_refs):
        out = mm_tn(place_both(cols, k, per_expert), xn)
        extra = mm_tn(place_one(bases[0], k, per_expert), carried[0])
        extra += mm_tn(place_one(bases[1], k, per_expert), carried[1])
        send_ref[:, LANES:] = out[:, LANES:].astype(BF16)
        send_ref[:, :LANES] = (out[:, :LANES] + extra).astype(BF16)


def expert_kernel(dims, *refs):
    dp, cp, dead = dims
    xs, cs = refs[:dp], refs[dp : 2 * dp]
    wu_ref, wd_ref = refs[2 * dp], refs[2 * dp + 1]
    outs = refs[2 * dp + 2 :]
    dx_refs, y_refs = outs[:dp], outs[dp : 2 * dp]
    h_ref, dpre_ref, dy_ref = outs[2 * dp :]
    rows = xs[0].shape[0]
    chunks = rows // cp
    wu, wd = wu_ref[0], wd_ref[0]
    lane = iota((rows, LANES), 1)
    row = iota((rows, LANES), 0)
    take = (iota((chunks, rows), 1) == iota((chunks, rows), 0) * cp + dead).astype(BF16)
    spread = (iota((rows, chunks), 0) // cp == iota((rows, chunks), 1)).astype(BF16)
    mine = jnp.logical_and(lane % cp == row % cp, lane < 3 * cp)
    mine_first = lane == row % cp
    target = iota((rows, rows), 1) // cp * cp + dead
    put_hi = (iota((rows, rows), 0) == target).astype(BF16)
    put_low = (iota((rows, rows), 0) == target + 1).astype(BF16)
    for j in range(dp):
        part = slice(j * rows, (j + 1) * rows)
        x = xs[j][...]
        cot = cs[j][...]
        carried = mm(spread, mm(take, x[:, :LANES]).astype(BF16))
        gate = jnp.sum(jnp.where(mine, carried, 0.0), axis=1, keepdims=True)
        cot32 = cot.astype(F32)
        dy = (cot32 * gate).astype(BF16)
        dy_ref[part, :] = dy
        pre = mm(x, wu)
        cdf = 0.5 * (1.0 + lax.erf(pre * INV_SQRT2))
        h = (pre * cdf).astype(BF16)
        h_ref[part, :] = h
        slope = cdf + pre * (jnp.exp(-0.5 * pre * pre) * INV_SQRT2PI)
        dpre = (mm(dy, wd) * slope).astype(BF16)
        dpre_ref[part, :] = dpre
        y = mm_nt(h, wd)
        y_refs[j][...] = y.astype(BF16)
        dg = jnp.sum(y * cot32, axis=1, keepdims=True)
        dg_hi = dg.astype(BF16).astype(F32)
        extra = mm(put_hi, jnp.where(mine_first, dg_hi, 0.0).astype(BF16))
        extra += mm(put_low, jnp.where(mine_first, dg - dg_hi, 0.0).astype(BF16))
        dx = mm_nt(dpre, wu)
        dx_refs[j][:, LANES:] = dx[:, LANES:].astype(BF16)
        dx_refs[j][:, :LANES] = (dx[:, :LANES] + extra).astype(BF16)


def expert_grad_kernel(dims, *refs):
    dp = dims
    xs = refs[:dp]
    h_ref, dpre_ref, dy_ref, gu_ref, gd_ref = refs[dp:]
    rows = xs[0].shape[0]
    gd_ref[...] = mm_tn(dy_ref[...], h_ref[...])
    acc = mm_tn(xs[0][...], dpre_ref[:rows, :])
    for j in range(1, dp):
        acc += mm_tn(xs[j][...], dpre_ref[j * rows : (j + 1) * rows, :])
    gu_ref[...] = acc


def add_kernel(dims, *refs):
    cp, dead = dims
    parts, out_ref = refs[:-1], refs[-1]
    acc = parts[0][...].astype(F32)
    for part in parts[1:]:
        acc += part[...].astype(F32)
    if dead is None:
        out_ref[...] = acc.astype(BF16)
        return
    out_ref[:, LANES:] = acc[:, LANES:].astype(BF16)
    first = acc[:, :LANES]
    rows = first.shape[0]
    place = iota((rows, LANES), 0) % cp
    both = first + pltpu.roll(first, rows - 1, 0)
    high = both.astype(BF16).astype(F32)
    low = pltpu.roll(both - high, 1, 0)
    out = jnp.where(place == dead, high, jnp.where(place == dead + 1, low, first))
    out_ref[:, :LANES] = out.astype(BF16)


def back_kernel(dims, *refs):
    seqs, groups, cp, dead, per_expert, local = dims
    rets = refs[:local]
    x1_ref, prob_ref, ids_ref, slot_ref, cot_ref = refs[local : local + 5]
    wo_ref, router_ref, gain_ref = refs[local + 5 : local + 8]
    dx1_ref, da_ref, do_ref, dl_ref, prod_ref = refs[local + 8 :]
    ids = ids_ref[...]
    probs = prob_ref[...]
    hot, total, gates = pick_probs(ids, probs)
    cols = [slot_ref[:, j : j + 1] for j in range(2)]
    rows = ids.shape[0]
    lane = iota((rows, LANES), 1)
    ranks = [col % cp for col in cols]
    moe = jnp.zeros(x1_ref.shape, F32)
    heads = [jnp.zeros((rows, LANES), F32) for _ in range(2)]
    for k in range(local):
        ret = rets[k][...]
        moe += mm(place_both(cols, k, per_expert), ret)
        for j in range(2):
            base = cols[j] - ranks[j] + dead
            heads[j] += mm(place_both([base, base + 1], k, per_expert), ret[:, :LANES])
    dg = [
        jnp.sum(jnp.where(lane == ranks[j], heads[j], 0.0), axis=1, keepdims=True) for j in range(2)
    ]
    mean_dg = dg[0] * gates[0] + dg[1] * gates[1]
    dprob = hot[0] * ((dg[0] - mean_dg) / total) + hot[1] * ((dg[1] - mean_dg) / total)
    dl = probs * (dprob - jnp.sum(probs * dprob, axis=1, keepdims=True))
    dl_ref[...] = dl
    router = router_ref[...]
    dl_hi = dl.astype(BF16)
    dl_low = (dl - dl_hi.astype(F32)).astype(BF16)
    dxn = moe + mm_nt(dl_hi, router) + mm_nt(dl_low, router)
    r, u = norm_parts(x1_ref[...])
    prod_ref[...] = (dxn * u).astype(BF16)
    scaled = dxn * gain_ref[...].astype(F32)
    dx1 = cot_ref[...].astype(F32) + r * (
        scaled - u * jnp.mean(u * scaled, axis=1, keepdims=True)
    )
    dx1_ref[...] = dx1
    da = dx1.astype(BF16)
    da_ref[...] = da
    width_h = do_ref.shape[2]
    each = rows // seqs
    for g in range(groups):
        block = mm_nt(da, wo_ref[g * width_h : (g + 1) * width_h, :]).astype(BF16)
        for m in range(seqs):
            do_ref[m * groups + g] = block[m * each : (m + 1) * each, :]


def small_grad_kernel(dims, o_ref, da_ref, xn_ref, dl_ref, prod_ref, out_ref):
    seqs, groups = dims
    width_h = o_ref.shape[2]
    rows, width = da_ref.shape
    each = rows // seqs
    experts = dl_ref.shape[1]
    for g in range(groups):
        count = min(width_h, width - g * width_h)
        if count <= 0:
            continue
        acc = jnp.zeros((width_h, width), F32)
        for m in range(seqs):
            acc += mm_tn(o_ref[m * groups + g], da_ref[m * each : (m + 1) * each, :])
        out_ref[g * width_h : g * width_h + count, :width] = acc[:count].astype(BF16)
    dl = dl_ref[...]
    dl_hi = dl.astype(BF16)
    dl_low = (dl - dl_hi.astype(F32)).astype(BF16)
    xn = xn_ref[...]
    tail = out_ref.shape[1] - width
    cut = (iota((experts, tail), 0) == iota((experts, tail), 1)).astype(BF16)
    router_part = mm_tn(xn, mm(dl_hi, cut).astype(BF16)) + mm_tn(xn, mm(dl_low, cut).astype(BF16))
    ones = (iota((rows, tail), 1) == experts).astype(BF16)
    out_ref[:, width:] = (router_part + mm_tn(prod_ref[...], ones)).astype(BF16)


def mixed_kernel(dims, *refs):
    per_expert, local = dims
    rets = refs[:local]
    x1_ref, prob_ref, ids_ref, slot_ref, out_ref = refs[local:]
    _, _, gates = pick_probs(ids_ref[...], prob_ref[...])
    out = x1_ref[...]
    for j in range(2):
        col = slot_ref[:, j : j + 1]
        y = mm(place_one(col, 0, per_expert), rets[0][...])
        for k in range(1, local):
            y += mm(place_one(col, k, per_expert), rets[k][...])
        out += gates[j] * y
    out_ref[...] = out.astype(BF16)


def last_kernel(dims, meta_ref, *refs):
    half, seqs, groups = dims
    parts = refs[:half]
    x_ref, dx1_ref, gain_ref, out_ref, acc_ref = refs[half:]
    z = meta_ref[0]
    rows = parts[0].shape[0]
    acc_ref[...] = jnp.zeros_like(acc_ref)
    for k in range(half):
        m = (2 * (z ^ k)) // groups
        acc_ref[m] += parts[k][...].astype(F32)
    gain = gain_ref[...]
    for m in range(seqs):
        part = slice(m * rows, (m + 1) * rows)
        x = x_ref[part, :].astype(F32)
        r = lax.rsqrt(jnp.mean(x * x, axis=1, keepdims=True) + EPS)
        u = x * r
        scaled = acc_ref[m] * gain
        back = r * (scaled - u * jnp.mean(u * scaled, axis=1, keepdims=True))
        out_ref[part, :] = (dx1_ref[part, :] + back).astype(BF16)


def permute_xor(value, axis, offset):
    count = lax.axis_size(axis)
    return lax.ppermute(value, axis, [(i, i ^ offset) for i in range(count)])


def spread_dp(value):
    return [value] + [permute_xor(value, "dp", j) for j in range(1, lax.axis_size("dp"))]


def swap_seq(value):
    return lax.all_to_all(value, "seq", split_axis=0, concat_axis=0, tiled=True)


def sum_shards(partial):
    dp = lax.axis_size("dp")
    rows, cols = partial.shape
    got = lax.all_to_all(
        partial.reshape(dp, rows // dp, cols), "dp", split_axis=0, concat_axis=0, tiled=True
    )
    return jnp.sum(got.astype(F32), axis=0).astype(BF16)


def shards(
    tokens,
    cotangent,
    expert_ids,
    buckets,
    gain_attn,
    w_qkv,
    rel_bias,
    w_attn_out,
    gain_moe,
    router,
    w_up,
    w_down,
):
    micro, batch, rows, width = tokens.shape
    heads = width // HD
    seqs = micro * batch
    seq, dp = lax.axis_size("seq"), lax.axis_size("dp")
    half = seq // 2
    length = seq * rows
    groups = seq // seqs
    hpd = -(-heads // groups)
    width_h = hpd * HD
    padded_heads = hpd * groups
    total = seqs * rows
    experts, local = router.shape[1], w_up.shape[0]
    slots = seqs * (expert_ids.shape[3] * rows // experts + 2)
    cp = -(-(slots + 2) // 8) * 8
    per_expert = seq * cp
    block = 256
    scale = 1.0 / math.sqrt(HD)
    shard = w_qkv.shape[0]
    me, dpi = lax.axis_index("seq"), lax.axis_index("dp")
    z, c = me // 2, me % 2
    meta = jnp.stack([z, c, dpi]).astype(jnp.int32)
    my_seq, my_group = me // groups, me % groups

    x_flat = tokens.reshape(seqs, rows, width)
    cot_flat = cotangent.reshape(total, width)
    ids_flat = expert_ids.reshape(total, expert_ids.shape[3])

    own, sib = [], []
    for k in range(half):
        target = (2 * (z ^ k)) // groups
        piece = lax.dynamic_index_in_dim(x_flat, target, 0, keepdims=False)
        if k:
            piece = permute_xor(piece, "seq", 2 * k)
        own.append(piece)
        sib.append(permute_xor(piece, "seq", 1))

    gain_lane = (3 * width_h) % LANES
    cols = 3 * width_h - gain_lane + LANES
    w_four = w_qkv.reshape(shard, 3, heads, HD)
    w_four = jnp.pad(w_four, ((0, 0), (0, 0), (0, padded_heads - heads), (0, 0)))
    w_groups = jnp.transpose(w_four.reshape(shard, 3, groups, width_h), (2, 0, 1, 3))
    w_groups = w_groups.reshape(groups, shard, 3 * width_h)
    gain_col = jnp.broadcast_to(gain_attn[None, :, None], (groups, shard, 1))
    w_groups = jnp.concatenate([w_groups, gain_col], axis=2)
    w_groups = jnp.pad(w_groups, ((0, 0), (0, 0), (0, cols - 3 * width_h - 1)))
    w_line = swap_seq(jnp.tile(w_groups, (seqs, 1, 1))).reshape(seq * shard, cols)
    w_parts = spread_dp(w_line)

    w_small = jnp.concatenate([w_attn_out, router, gain_moe[:, None]], axis=1)
    small_cols = -(-w_small.shape[1] // LANES) * LANES
    w_small = jnp.pad(w_small, ((0, 0), (0, small_cols - w_small.shape[1])))
    w_small = lax.all_gather(w_small, ("dp", "seq"), axis=0, tiled=True)
    w_out = w_small[:, :width]
    w_out_rows = jnp.pad(w_out, ((0, groups * width_h - width), (0, 0)))
    router_all = w_small[:, width : width + experts]
    gain_second = w_small[:, width + experts].reshape(1, width)

    hot = (buckets[:, None] == jnp.arange(rel_bias.shape[0], dtype=jnp.int32)).astype(F32)
    table = jnp.pad(rel_bias.astype(F32), ((0, 0), (0, padded_heads - heads)))
    table = lax.dynamic_slice_in_dim(table, my_group * hpd, hpd, 1)
    by_distance = jnp.einsum("tn,nh->ht", hot, table, precision=lax.Precision.HIGHEST)
    bias_rev = jnp.concatenate(
        [jnp.flip(by_distance, axis=1), jnp.full((hpd, block), NEG, F32)], axis=1
    )

    slot_cols, *cot_send = call(
        functools.partial(route_kernel, (total, experts, local, seq, cp)),
        [((total, LANES), jnp.int32)] + [((per_expert, width), BF16)] * local,
        [ids_flat, cot_flat],
        name="route",
    )

    def to_experts(value):
        got = swap_seq(value.reshape(seq, cp, width)).reshape(per_expert, width)
        return spread_dp(got)

    o_all, qkv, xn1, w_mine, lse, slab, gain_first = call(
        functools.partial(attn_fwd_kernel, (half, dp, hpd, block, gain_lane, scale)),
        [
            ((length, width_h), BF16),
            ((length, cols), BF16),
            ((length, width), BF16),
            ((width, cols), BF16),
            ((length, LANES), F32),
            ((hpd, block, length), F32),
            ((1, width), F32),
        ],
        [meta] + own + sib + w_parts + [bias_rev],
        smem=1,
        name="attn_fwd",
    )
    cot_parts = [to_experts(value) for value in cot_send]
    o_mine = swap_seq(o_all.reshape(seq, rows, width_h))
    x1, xn2, probs, *send = call(
        functools.partial(mid_kernel, (seqs, groups, cp, slots, per_expert)),
        [((total, width), F32), ((total, width), BF16), ((total, experts), F32)]
        + [((per_expert, width), BF16)] * local,
        [
            o_mine,
            x_flat.reshape(total, width),
            w_out_rows,
            router_all,
            gain_second,
            ids_flat,
            slot_cols,
        ],
        name="mid",
    )

    slot_parts = [to_experts(value) for value in send]
    ret_dx, ret_y, grads_up, grads_down = [], [], [], []
    for e in range(local):
        outs = call(
            functools.partial(expert_kernel, (dp, cp, slots)),
            [((per_expert, width), BF16)] * (2 * dp)
            + [((dp * per_expert, w_up.shape[2]), BF16)] * 2
            + [((dp * per_expert, width), BF16)],
            slot_parts[e] + cot_parts[e] + [w_up[e : e + 1], w_down[e : e + 1]],
            name="expert",
        )
        dx_parts, y_parts = outs[:dp], outs[dp : 2 * dp]
        hidden, dpre, dy = outs[2 * dp :]
        dx_got = [dx_parts[0]] + [permute_xor(dx_parts[j], "dp", j) for j in range(1, dp)]
        (dx_sum,) = call(
            functools.partial(add_kernel, (cp, slots)),
            [((per_expert, width), BF16)],
            dx_got,
            name="add_dx",
        )
        ret_dx.append(swap_seq(dx_sum.reshape(seq, cp, width)).reshape(per_expert, width))
        g_up, g_down = call(
            functools.partial(expert_grad_kernel, dp),
            [((width, w_up.shape[2]), F32)] * 2,
            slot_parts[e] + [hidden, dpre, dy],
            name="expert_grad",
        )
        grads_up.append(g_up)
        grads_down.append(g_down)
        ret_y.append(y_parts)

    dx1, da, do_send, dlogits, prod = call(
        functools.partial(back_kernel, (seqs, groups, cp, slots, per_expert, local)),
        [
            ((total, width), F32),
            ((total, width), BF16),
            ((seq, rows, width_h), BF16),
            ((total, experts), F32),
            ((total, width), BF16),
        ],
        ret_dx
        + [x1, probs, ids_flat, slot_cols, cot_flat, w_out_rows, router_all, gain_second],
        name="back",
    )
    do_all = swap_seq(do_send).reshape(length, width_h)

    mixed_in = []
    for e in range(local):
        y_parts = ret_y[e]
        y_got = [y_parts[0]] + [permute_xor(y_parts[j], "dp", j) for j in range(1, dp)]
        (y_sum,) = call(
            functools.partial(add_kernel, (cp, None)),
            [((per_expert, width), BF16)],
            y_got,
            name="add_y",
        )
        mixed_in.append(swap_seq(y_sum.reshape(seq, cp, width)).reshape(per_expert, width))
    (mixed,) = call(
        functools.partial(mixed_kernel, (per_expert, local)),
        [((total, width), BF16)],
        mixed_in + [x1, probs, ids_flat, slot_cols],
        name="mixed",
    )

    (small,) = call(
        functools.partial(small_grad_kernel, (seqs, groups)),
        [((width, small_cols), BF16)],
        [o_mine, da, xn2, dlogits, prod],
        name="small_grad",
    )
    small = swap_seq(sum_shards(small).reshape(seq, shard, small_cols))
    small = jnp.sum(small.astype(F32), axis=0)

    span = length + block
    dx_own, dx_sib, grad_cols, grad_rev = call(
        functools.partial(attn_bwd_kernel, (half, hpd, block, scale)),
        [
            ((half, rows, width), BF16),
            ((half, rows, width), BF16),
            ((width, cols), BF16),
            ((hpd, span), F32),
        ],
        [meta, do_all, qkv, xn1, w_mine, lse, slab],
        scratch=[
            pltpu.VMEM((length, cols), BF16),
            pltpu.VMEM((length, HD), F32),
            pltpu.VMEM((length, HD), F32),
            pltpu.VMEM((block, span), F32),
        ],
        smem=1,
        name="attn_bwd",
    )
    dx_parts = []
    for k in range(half):
        both = dx_own[k].astype(F32) + permute_xor(dx_sib[k], "seq", 1).astype(F32)
        both = both.astype(BF16)
        dx_parts.append(permute_xor(both, "seq", 2 * k) if k else both)
    (grad_tokens,) = call(
        functools.partial(last_kernel, (half, seqs, groups)),
        [((total, width), BF16)],
        [meta] + dx_parts + [x_flat.reshape(total, width), dx1, gain_first],
        scratch=[pltpu.VMEM((seqs, rows, width), F32)],
        smem=1,
        name="last",
    )

    line = swap_seq(sum_shards(grad_cols).reshape(seq, shard, cols))
    line = jnp.sum(line.astype(F32).reshape(seqs, groups, shard, cols), axis=0)
    line = line[:, :, : 3 * width_h].reshape(groups, shard, 3, width_h)
    grad_qkv = jnp.transpose(line, (1, 2, 0, 3)).reshape(shard, 3, groups * width_h)
    grad_qkv = grad_qkv[:, :, :width].reshape(shard, 3 * width)
    grad_gain_attn = jnp.sum(grad_qkv * w_qkv.astype(F32), axis=1) / gain_attn.astype(F32)

    by_distance_grad = jnp.flip(grad_rev[:, :length], axis=1)
    table_part = jnp.einsum("tn,ht->nh", hot, by_distance_grad, precision=lax.Precision.HIGHEST)
    table_grad = jnp.zeros((rel_bias.shape[0], padded_heads), F32)
    table_grad = lax.dynamic_update_slice_in_dim(table_grad, table_part, my_group * hpd, 1)
    table_grad = lax.psum(table_grad[:, :heads], ("dp", "seq"))

    return (
        mixed.reshape(tokens.shape),
        grad_tokens.reshape(tokens.shape),
        grad_gain_attn,
        grad_qkv,
        table_grad,
        small[:, :width],
        small[:, width + experts],
        small[:, width : width + experts],
        jnp.stack(grads_up),
        jnp.stack(grads_down),
    )


def solution(mesh):
    in_specs = (
        P(None, "dp", "seq", None),
        P(None, "dp", "seq", None),
        P(None, "dp", "seq", None),
        P(),
        P(("dp", "seq")),
        P(("dp", "seq"), None),
        P(),
        P(("dp", "seq"), None),
        P(("dp", "seq")),
        P(("dp", "seq"), None),
        P("seq", None, "dp"),
        P("seq", None, "dp"),
    )
    out_specs = (
        P(None, "dp", "seq", None),
        P(None, "dp", "seq", None),
        P(("dp", "seq")),
        P(("dp", "seq"), None),
        P(),
        P(("dp", "seq"), None),
        P(("dp", "seq")),
        P(("dp", "seq"), None),
        P("seq", None, "dp"),
        P("seq", None, "dp"),
    )
    return jax.shard_map(shards, mesh=mesh, in_specs=in_specs, out_specs=out_specs, check_vma=False)
```

```python
import functools
import math

import jax
import jax.numpy as jnp
from jax import lax
from jax.experimental import pallas as pl
from jax.experimental.pallas import tpu as pltpu
from jax.sharding import Mesh
from jax.sharding import PartitionSpec as P

HD = 64
LANES = 128
EPS = 1e-06
NEG = -1e30
F32 = jnp.float32
BF16 = jnp.bfloat16
VMEM_BYTES = 56 * 1024 * 1024
INV_SQRT2 = 1.0 / math.sqrt(2.0)
INV_SQRT2PI = 1.0 / math.sqrt(2.0 * math.pi)


def mm(a, b):
    return lax.dot_general(a, b, (((1,), (0,)), ((), ())), preferred_element_type=F32)


def mm_nt(a, b):
    return lax.dot_general(a, b, (((1,), (1,)), ((), ())), preferred_element_type=F32)


def mm_tn(a, b):
    return lax.dot_general(a, b, (((0,), (0,)), ((), ())), preferred_element_type=F32)


def iota(shape, dim):
    return lax.broadcasted_iota(jnp.int32, shape, dim)


def split3(v):
    hi = v.astype(BF16).astype(F32)
    rest = v - hi
    mid = rest.astype(BF16).astype(F32)
    return hi, mid, rest - mid


def call(kernel, outs, ins, scratch=(), smem=0, name=None, after=()):
    spec = [pl.BlockSpec(memory_space=pltpu.SMEM)] * smem
    spec += [pl.BlockSpec(memory_space=pltpu.VMEM)] * (len(ins) - smem)
    spec += [pl.BlockSpec(memory_space=pl.ANY)] * len(after)
    count = len(ins)

    def body(*refs):
        kernel(*refs[:count], *refs[count + len(after) :])

    return pl.pallas_call(
        body,
        out_shape=[jax.ShapeDtypeStruct(s, d) for s, d in outs],
        in_specs=spec,
        out_specs=[pl.BlockSpec(memory_space=pltpu.VMEM)] * len(outs),
        scratch_shapes=list(scratch),
        compiler_params=pltpu.CompilerParams(vmem_limit_bytes=VMEM_BYTES),
        cost_estimate=pl.CostEstimate(flops=0, transcendentals=0, bytes_accessed=1),
        name=name,
    )(*ins, *after)


def route_kernel(dims, meta_ref, ids_ref, cot_ref, slot_ref, out_ref):
    rows, experts, local, seq, cp = dims
    ids = ids_ref[...]
    expert = iota((rows, experts), 1)
    hot = [(ids[:, j : j + 1] == expert).astype(F32) for j in range(2)]
    before = (iota((rows, rows), 0) > iota((rows, rows), 1)).astype(BF16)
    rank = mm(before, (hot[0] + hot[1]).astype(BF16))
    cols = []
    for j in range(2):
        own = jnp.sum(hot[j] * rank, axis=1, keepdims=True).astype(jnp.int32)
        e = ids[:, j : j + 1]
        cols.append(((e % local) ^ meta_ref[3]) * (seq * cp) + (e // local) * cp + own)
    lane = iota((rows, LANES), 1)
    slot_ref[...] = jnp.where(lane == 0, cols[0], cols[1])
    place = place_both([merged(col, cp, seq * cp) for col in cols], 0, 2 * seq * cp)
    out_ref[...] = mm_tn(place, cot_ref[...]).astype(BF16)


def merged(col, cp, per_expert):
    inside = col % per_expert
    return inside // cp * (2 * cp) + col // per_expert * cp + inside % cp


def place_one(col, e, count):
    return (iota((col.shape[0], count), 1) + e * count == col).astype(BF16)


def place_both(cols, e, count):
    where = iota((cols[0].shape[0], count), 1) + e * count
    return jnp.logical_or(where == cols[0], where == cols[1]).astype(BF16)


def attn_fwd_kernel(dims, meta_ref, *refs):
    half, dp, hpd, block, gain_lane, scale = dims
    own, sib, wp = refs[:half], refs[half : 2 * half], refs[2 * half : 2 * half + dp]
    brev_ref = refs[2 * half + dp]
    o_ref, qkv_ref, xn_ref, w_ref, lse_ref, slab_ref, gain_ref = refs[2 * half + dp + 1 :]
    z, c, d = meta_ref[0], meta_ref[1], meta_ref[2]
    part = wp[0].shape[0]
    for j in range(dp):
        w_ref[pl.ds(pl.multiple_of((d ^ j) * part, part), part), :] = wp[j][...]
    tile = 3 * hpd * HD // LANES * LANES
    turned = jnp.transpose(w_ref[:, tile : tile + LANES].astype(F32))
    gain = turned[gain_lane : gain_lane + 1, :]
    gain_ref[...] = gain
    rows = own[0].shape[0]
    for group, core in ((own, c), (sib, 1 - c)):
        for k in range(half):
            x = group[k][...].astype(F32)
            r = lax.rsqrt(jnp.mean(x * x, axis=1, keepdims=True) + EPS)
            start = pl.multiple_of((2 * (z ^ k) + core) * rows, rows)
            xn_ref[pl.ds(start, rows), :] = (x * r * gain).astype(BF16)
    length = xn_ref.shape[0]
    for i in range(length // block):
        part_rows = slice(i * block, (i + 1) * block)
        qkv_ref[part_rows, :] = mm(xn_ref[part_rows, :], w_ref[...]).astype(BF16)
    span = length + block
    width_h = hpd * HD
    for h in range(hpd):
        base = brev_ref[h : h + 1, :]
        rolled = [base if i == 7 else pltpu.roll(base, span - (7 - i), 1) for i in range(8)]
        slab = jnp.concatenate(rolled, axis=0)
        n = 8
        while n < block:
            slab = jnp.concatenate([pltpu.roll(slab, span - n, 1), slab], axis=0)
            n *= 2
        slab_ref[h] = slab[:, :length]
    lane = iota((block, LANES), 1)
    for i in range(length // block):
        q_rows = slice(i * block, (i + 1) * block)
        keys = (i + 1) * block
        lse = jnp.zeros((block, LANES), F32)
        for h in range(hpd):
            q = qkv_ref[q_rows, h * HD : (h + 1) * HD] * jnp.asarray(scale, BF16)
            k = qkv_ref[:keys, width_h + h * HD : width_h + (h + 1) * HD]
            v = qkv_ref[:keys, 2 * width_h + h * HD : 2 * width_h + (h + 1) * HD]
            s = mm_nt(q, k) + slab_ref[h, :, length - keys :]
            top = jnp.max(s, axis=1, keepdims=True)
            e = jnp.exp(s - top)
            total = jnp.sum(e, axis=1, keepdims=True)
            p = (e * (1.0 / total)).astype(BF16)
            o_ref[q_rows, h * HD : (h + 1) * HD] = mm(p, v).astype(BF16)
            lse = jnp.where(lane == h, top + jnp.log(total), lse)
        lse_ref[q_rows, :] = lse


def three_parts(table, width):
    wide = jnp.concatenate(list(split3(table)), axis=1)
    if width > 3 * LANES:
        wide = jnp.concatenate([wide, jnp.zeros((8, width - 3 * LANES), F32)], axis=1)
    return jnp.concatenate([wide, jnp.zeros_like(wide)], axis=0).astype(BF16)


def attn_bwd_kernel(dims, meta_ref, do_ref, qkv_ref, w_ref, lse_ref, slab_ref, *refs):
    half, hpd, block, scale, buckets = dims
    hot_ref, dx_own, dx_sib, dqkv_ref, table_ref, dk_ref, dv_ref, db_ref, gb_ref = refs
    gb_ref[...] = jnp.zeros_like(gb_ref)
    z, c = meta_ref[0], meta_ref[1]
    length = qkv_ref.shape[0]
    width_h = hpd * HD
    blocks = length // block
    dqkv_ref[...] = jnp.zeros_like(dqkv_ref)
    for h in range(hpd):
        cols = slice(h * HD, (h + 1) * HD)
        k_cols = slice(width_h + h * HD, width_h + (h + 1) * HD)
        v_cols = slice(2 * width_h + h * HD, 2 * width_h + (h + 1) * HD)
        for i in range(blocks - 1, -1, -1):
            rows = slice(i * block, (i + 1) * block)
            keys = (i + 1) * block
            q = qkv_ref[rows, cols] * jnp.asarray(scale, BF16)
            k = qkv_ref[:keys, k_cols]
            v = qkv_ref[:keys, v_cols]
            do = do_ref[rows, cols]
            s = mm_nt(q, k) + slab_ref[h, :, length - keys :]
            p = jnp.exp(s - lse_ref[rows, h : h + 1])
            dprob = mm_nt(do, v)
            delta = jnp.sum(p * dprob, axis=1, keepdims=True)
            ds32 = p * (dprob - delta)
            ds = ds32.astype(BF16)
            dqkv_ref[rows, cols] = (mm(ds, k) * scale).astype(BF16)
            dk = mm_tn(ds, q)
            dv = mm_tn(p.astype(BF16), do)
            if i == blocks - 1:
                dk_ref[...] = dk
                dv_ref[...] = dv
                db_ref[:, :length] = ds.astype(F32)
            else:
                dk_ref[:keys, :] += dk
                dv_ref[:keys, :] += dv
                db_ref[:, length - keys : length] += ds.astype(F32)
        dqkv_ref[:, k_cols] = dk_ref[...].astype(BF16)
        dqkv_ref[:, v_cols] = dv_ref[...].astype(BF16)
        db_ref[:, length:] = jnp.zeros((block, block), F32)
        n = block
        acc = db_ref[...]
        while n > 1:
            n //= 2
            acc = pltpu.roll(acc[:n], n, 1) + acc[n:]
        gb_ref[h : h + 1, :] = acc
    hot = hot_ref[...]
    hi, mid, low = split3(gb_ref[...])
    by_bucket = mm(hi.astype(BF16), hot) + mm(mid.astype(BF16), hot) + mm(low.astype(BF16), hot)
    table = jnp.zeros((8, LANES), F32)
    row, lane = iota((8, LANES), 0), iota((8, LANES), 1)
    for h in range(hpd):
        head = meta_ref[4] * hpd + h
        here = jnp.logical_and(row == head % 8, lane // buckets == head // 8)
        table = jnp.where(here, by_bucket[h : h + 1, :], table)
    table_ref[...] = table
    rows = dx_own.shape[1]
    w = w_ref[...]
    for out_ref, core in ((dx_own, c), (dx_sib, 1 - c)):
        for k in range(half):
            start = pl.multiple_of((2 * (z ^ k) + core) * rows, rows)
            out_ref[k] = mm_nt(dqkv_ref[pl.ds(start, rows), :], w).astype(BF16)


def cols_kernel(dims, meta_ref, xn_ref, dqkv_ref, table_ref, *refs):
    gq_refs, gq_ref = refs[:-1], refs[-1]
    gq_ref[...] = mm_tn(xn_ref[...], dqkv_ref[...]).astype(BF16)
    table = three_parts(table_ref[...], gq_ref.shape[1])
    part = gq_refs[0].shape[0] - 16
    for j, piece in enumerate(gq_refs):
        start = pl.multiple_of((meta_ref[2] ^ j) * part, part)
        piece[:part, :] = gq_ref[pl.ds(start, part), :]
        piece[part:, :] = table


def pick_probs(ids, probs):
    expert = iota(probs.shape, 1)
    hot = [(ids[:, j : j + 1] == expert).astype(F32) for j in range(2)]
    picked = [jnp.sum(probs * one, axis=1, keepdims=True) for one in hot]
    total = picked[0] + picked[1]
    return hot, total, [one / total for one in picked]


def norm_parts(x1):
    r = lax.rsqrt(jnp.mean(x1 * x1, axis=1, keepdims=True) + EPS)
    return r, x1 * r


def head_rows(groups, width_h, width):
    return [(g, min(width_h, width - g * width_h)) for g in range(groups) if g * width_h < width]


def mid_kernel(dims, o_ref, x_ref, ids_ref, slot_ref, *refs):
    seqs, groups, cp, dead, per_expert, experts = dims
    ws_ref, x1_ref, xn_ref, prob_ref, gain_ref, send_ref = refs
    width = x_ref.shape[1]
    lane_at = width + experts
    tile = lane_at // LANES * LANES
    turned = jnp.transpose(ws_ref[:, tile : tile + LANES].astype(F32))
    gain = turned[lane_at - tile : lane_at - tile + 1, :]
    gain_ref[...] = gain
    rows = x_ref.shape[0] // seqs
    width_h = o_ref.shape[2]
    for m in range(seqs):
        part = slice(m * rows, (m + 1) * rows)
        acc = x_ref[part, :].astype(F32)
        for g, count in head_rows(groups, width_h, width):
            w_rows = ws_ref[g * width_h : g * width_h + count, :width]
            acc += mm(o_ref[m * groups + g][:, :count], w_rows)
        x1_ref[part, :] = acc
    r, u = norm_parts(x1_ref[...])
    xn = (u * gain).astype(BF16)
    xn_ref[...] = xn
    logits = mm(xn, ws_ref[:, width : width + experts])
    e = jnp.exp(logits - jnp.max(logits, axis=1, keepdims=True))
    probs = e / jnp.sum(e, axis=1, keepdims=True)
    prob_ref[...] = probs
    ids = ids_ref[...]
    _, _, gates = pick_probs(ids, probs)
    cols = [slot_ref[:, j : j + 1] for j in range(2)]
    lane = iota((xn.shape[0], LANES), 1)
    places = [merged(col, cp, per_expert) for col in cols]
    out = mm_tn(place_both(places, 0, 2 * per_expert), xn)
    extra = jnp.zeros((2 * per_expert, LANES), F32)
    for j in range(2):
        rank = cols[j] % cp
        hi, mid, low = split3(gates[j])
        value = jnp.where(lane < cp, hi, jnp.where(lane < 2 * cp, mid, low))
        keep = jnp.logical_and(lane % cp == rank, lane < 3 * cp)
        carried = jnp.where(keep, value, 0.0).astype(BF16)
        extra += mm_tn(place_one(places[j] - rank + dead, 0, 2 * per_expert), carried)
    send_ref[:, LANES:] = out[:, LANES:].astype(BF16)
    send_ref[:, :LANES] = (out[:, :LANES] + extra).astype(BF16)


def expert_kernel(dims, *refs):
    count, cp, dead = dims
    xs, cs = refs[:count], refs[count : 2 * count]
    weights = refs[2 * count : 2 * count + 4]
    outs = refs[2 * count + 4 :]
    dx_refs = outs[:count]
    h_refs, dpre_refs, dy_ref = outs[count : count + 2], outs[count + 2 : count + 4], outs[count + 4]
    rows = xs[0].shape[0]
    chunks = rows // cp
    lane = iota((rows, LANES), 1)
    row = iota((rows, LANES), 0)
    take = (iota((chunks, rows), 1) == iota((chunks, rows), 0) * cp + dead).astype(BF16)
    spread = (iota((rows, chunks), 0) // cp == iota((rows, chunks), 1)).astype(BF16)
    mine = jnp.logical_and(lane % cp == row % cp, lane < 3 * cp)
    mine_first = lane == row % cp
    target = iota((rows, rows), 1) // cp * cp + dead
    put_hi = (iota((rows, rows), 0) == target).astype(BF16)
    put_low = (iota((rows, rows), 0) == target + 1).astype(BF16)
    for j in range(count):
        part = slice(j * rows, (j + 1) * rows)
        x = xs[j][...]
        cot = cs[j][...]
        carried = mm(spread, mm(take, x[:, :LANES]).astype(BF16))
        gate = jnp.sum(jnp.where(mine, carried, 0.0), axis=1, keepdims=True)
        dy_ref[part, :] = (cot.astype(F32) * gate).astype(BF16)
        dg = jnp.zeros((rows, 1), F32)
        dx = jnp.zeros((rows, x.shape[1]), F32)
        for f in range(2):
            pre = mm(x, weights[2 * f][...])
            cdf = 0.5 * (1.0 + lax.erf(pre * INV_SQRT2))
            hidden = pre * cdf
            h_refs[f][part, :] = hidden.astype(BF16)
            slope = cdf + pre * (jnp.exp(-0.5 * pre * pre) * INV_SQRT2PI)
            dh = mm(cot, weights[2 * f + 1][...])
            dg += jnp.sum(hidden * dh, axis=1, keepdims=True)
            dpre = (dh * slope * gate).astype(BF16)
            dpre_refs[f][part, :] = dpre
            dx += mm_nt(dpre, weights[2 * f][...])
        dg_hi = dg.astype(BF16).astype(F32)
        extra = mm(put_hi, jnp.where(mine_first, dg_hi, 0.0).astype(BF16))
        extra += mm(put_low, jnp.where(mine_first, dg - dg_hi, 0.0).astype(BF16))
        dx_refs[j][:, LANES:] = dx[:, LANES:].astype(BF16)
        dx_refs[j][:, :LANES] = (dx[:, :LANES] + extra).astype(BF16)


def up_grad_kernel(dims, *refs):
    calls, count = dims
    xs, dpre, out_ref = refs[: calls * count], refs[calls * count : -1], refs[-1]
    rows = xs[0].shape[0]
    acc = None
    for i in range(calls):
        for j in range(count):
            term = mm_tn(xs[i * count + j][...], dpre[i][j * rows : (j + 1) * rows, :])
            acc = term if acc is None else acc + term
    out_ref[...] = acc.astype(out_ref.dtype)


def expert_out_kernel(dims, *refs):
    calls, count = dims
    hidden, weights, outs = refs[: 2 * calls], refs[2 * calls : 2 * calls + 2], refs[2 * calls + 2 :]
    rows = outs[0].shape[0]
    for i in range(calls):
        for j in range(count):
            part = slice(j * rows, (j + 1) * rows)
            y = mm_nt(hidden[2 * i][part, :], weights[0][...])
            y += mm_nt(hidden[2 * i + 1][part, :], weights[1][...])
            outs[i * count + j][...] = y.astype(BF16)


def down_grad_kernel(dims, *refs):
    calls = dims
    saved, outs = refs[: 3 * calls], refs[3 * calls :]
    for f in range(2):
        acc = mm_tn(saved[2][...], saved[f][...])
        for i in range(1, calls):
            acc += mm_tn(saved[3 * i + 2][...], saved[3 * i + f][...])
        outs[f][...] = acc.astype(outs[f].dtype)


def both_experts_kernel(dims, meta_ref, up_ref, up_pair, down_ref, down_pair, out_up, out_down):
    bit = meta_ref[3]
    for own, pair, out in ((up_ref, up_pair, out_up), (down_ref, down_pair, out_down)):
        out[bit] = own[...]
        out[1 - bit] = pair[1 - bit].astype(F32)


def merge_kernel(dims, *refs):
    dp, shard = dims
    lines, smalls, out_ref, acc_ref = refs[:dp], refs[dp : 2 * dp], refs[2 * dp], refs[2 * dp + 1]
    part = smalls[0].shape[0]
    cols = lines[0].shape[1]
    table = jnp.zeros((8, LANES), F32)
    acc = jnp.zeros((part, cols), F32)
    small = jnp.zeros(smalls[0].shape, F32)
    for j in range(dp):
        acc += lines[j][:part, :].astype(F32)
        tail = lines[j][part:, :].astype(F32)[:8]
        table += sum(tail[:, i * LANES : (i + 1) * LANES] for i in range(3))
        small += smalls[j][...].astype(F32)
    acc_ref[:, :cols] = acc
    acc_ref[:, cols:] = small
    width = acc_ref.shape[1]
    rows = out_ref.shape[1]
    tail = jnp.concatenate(list(split3(table)), axis=1)
    tail = jnp.concatenate([tail, jnp.zeros((8, width - 3 * LANES), F32)], axis=1)
    fill = rows - 8 - shard
    for s in range(out_ref.shape[0]):
        block = [acc_ref[s * shard : (s + 1) * shard, :], tail]
        if fill:
            block = [block[0], jnp.zeros((fill, width), F32), tail]
        out_ref[s] = jnp.concatenate(block, axis=0).astype(BF16)


def finish_kernel(dims, got_ref, w_ref, gain_ref, *outs):
    seqs, groups, hpd, cols, experts = dims
    qkv_ref, out_ref, router_ref, first_ref, second_ref, table_ref = outs
    width_h = hpd * HD
    shard, width = w_ref.shape[0], w_ref.shape[1] // 3
    got = [got_ref[s].astype(F32) for s in range(seqs * groups)]
    whole = functools.reduce(jnp.add, got)
    last = whole.shape[0] - 8
    table_ref[...] = sum(whole[last:, i * LANES : (i + 1) * LANES] for i in range(3))
    small = whole[:shard, cols:]
    out_ref[...] = small[:, :width]
    router_ref[...] = small[:, width : width + experts]
    tile = (width + experts) // LANES * LANES
    turned = jnp.transpose(pad_rows(small[:, tile : tile + LANES]))
    second_ref[...] = turned[width + experts - tile :][:1, :shard]
    for g, count in head_rows(groups, width_h, width):
        acc = functools.reduce(jnp.add, [got[m * groups + g][:shard, :cols] for m in range(seqs)])
        for i in range(3):
            start = i * width + g * width_h
            qkv_ref[:, start : start + count] = acc[:, i * width_h : i * width_h + count]
    total = jnp.sum(qkv_ref[...] * w_ref[...].astype(F32), axis=1, keepdims=True)
    total = jnp.broadcast_to(total / gain_ref[...].astype(F32), (shard, LANES))
    first_ref[...] = jnp.transpose(pad_rows(total))[:1, :shard]


def pad_rows(value):
    count = LANES - value.shape[0]
    return jnp.concatenate([value, jnp.zeros((count, value.shape[1]), F32)], axis=0)


def add_kernel(dims, *refs):
    cp, dead = dims
    parts, out_ref = refs[:-1], refs[-1]
    acc = parts[0][...].astype(F32)
    for part in parts[1:]:
        acc += part[...].astype(F32)
    if dead is None:
        out_ref[...] = acc.astype(BF16)
        return
    out_ref[:, LANES:] = acc[:, LANES:].astype(BF16)
    first = acc[:, :LANES]
    rows = first.shape[0]
    place = iota((rows, LANES), 0) % cp
    both = first + pltpu.roll(first, rows - 1, 0)
    high = both.astype(BF16).astype(F32)
    low = pltpu.roll(both - high, 1, 0)
    out = jnp.where(place == dead, high, jnp.where(place == dead + 1, low, first))
    out_ref[:, :LANES] = out.astype(BF16)


def add_both_kernel(dims, *refs):
    count = (len(refs) - 2) // 2
    for i in range(2):
        acc = refs[i * count][...].astype(F32)
        for part in refs[i * count + 1 : (i + 1) * count]:
            acc += part[...].astype(F32)
        refs[2 * count + i][...] = acc.astype(BF16)


def back_kernel(dims, *refs):
    seqs, groups, cp, dead, per_expert, local = dims
    rets = refs[:local]
    x1_ref, prob_ref, ids_ref, slot_ref, cot_ref = refs[local : local + 5]
    ws_ref, gain_ref = refs[local + 5 : local + 7]
    dx1_ref, da_ref, do_ref, dl_ref, prod_ref = refs[local + 7 :]
    width = x1_ref.shape[1]
    ids = ids_ref[...]
    probs = prob_ref[...]
    hot, total, gates = pick_probs(ids, probs)
    cols = [slot_ref[:, j : j + 1] for j in range(2)]
    rows = ids.shape[0]
    lane = iota((rows, LANES), 1)
    ranks = [col % cp for col in cols]
    moe = jnp.zeros(x1_ref.shape, F32)
    heads = [jnp.zeros((rows, LANES), F32) for _ in range(2)]
    for k in range(local):
        ret = rets[k][...]
        moe += mm(place_both(cols, k, per_expert), ret)
        for j in range(2):
            base = cols[j] - ranks[j] + dead
            heads[j] += mm(place_both([base, base + 1], k, per_expert), ret[:, :LANES])
    dg = [
        jnp.sum(jnp.where(lane == ranks[j], heads[j], 0.0), axis=1, keepdims=True) for j in range(2)
    ]
    mean_dg = dg[0] * gates[0] + dg[1] * gates[1]
    dprob = hot[0] * ((dg[0] - mean_dg) / total) + hot[1] * ((dg[1] - mean_dg) / total)
    dl = probs * (dprob - jnp.sum(probs * dprob, axis=1, keepdims=True))
    dl_ref[...] = dl
    router = ws_ref[:, width : width + probs.shape[1]]
    dl_hi = dl.astype(BF16)
    dl_low = (dl - dl_hi.astype(F32)).astype(BF16)
    dxn = moe + mm_nt(dl_hi, router) + mm_nt(dl_low, router)
    r, u = norm_parts(x1_ref[...])
    prod_ref[...] = (dxn * u).astype(BF16)
    scaled = dxn * gain_ref[...]
    dx1 = cot_ref[...].astype(F32) + r * (
        scaled - u * jnp.mean(u * scaled, axis=1, keepdims=True)
    )
    dx1_ref[...] = dx1
    da = dx1.astype(BF16)
    da_ref[...] = da
    width_h = do_ref.shape[2]
    each = rows // seqs
    used = head_rows(groups, width_h, width)
    if len(used) < groups or used[-1][1] < width_h:
        do_ref[...] = jnp.zeros_like(do_ref)
    for g, count in used:
        block = mm_nt(da, ws_ref[g * width_h : g * width_h + count, :width]).astype(BF16)
        for m in range(seqs):
            do_ref[m * groups + g, :, :count] = block[m * each : (m + 1) * each, :]


def side_kernel(dims, first_ref, second_ref, out_ref):
    both = [first_ref[...].astype(F32), second_ref[...].astype(F32)]
    out_ref[...] = jnp.concatenate(both, axis=1).astype(BF16)


def pair_kernel(dims, own_ref, got_ref, *outs):
    for k, out_ref in enumerate(outs):
        out_ref[...] = (own_ref[k].astype(F32) + got_ref[k].astype(F32)).astype(BF16)


def small_grad_kernel(dims, meta_ref, o_ref, da_ref, xn_ref, dl_ref, prod_ref, *refs):
    seqs, groups = dims
    pieces, out_ref = refs[:-1], refs[-1]
    width_h = o_ref.shape[2]
    rows, width = da_ref.shape
    each = rows // seqs
    experts = dl_ref.shape[1]
    for g, count in head_rows(groups, width_h, width):
        acc = jnp.zeros((width_h, width), F32)
        for m in range(seqs):
            acc += mm_tn(o_ref[m * groups + g], da_ref[m * each : (m + 1) * each, :])
        out_ref[g * width_h : g * width_h + count, :width] = acc[:count].astype(BF16)
    dl = dl_ref[...]
    dl_hi = dl.astype(BF16)
    dl_low = (dl - dl_hi.astype(F32)).astype(BF16)
    xn = xn_ref[...]
    tail = out_ref.shape[1] - width
    cut = (iota((experts, tail), 0) == iota((experts, tail), 1)).astype(BF16)
    router_part = mm_tn(xn, mm(dl_hi, cut).astype(BF16)) + mm_tn(xn, mm(dl_low, cut).astype(BF16))
    ones = (iota((rows, tail), 1) == experts).astype(BF16)
    out_ref[:, width:] = (router_part + mm_tn(prod_ref[...], ones)).astype(BF16)
    part = pieces[0].shape[0]
    for j, piece in enumerate(pieces):
        start = pl.multiple_of((meta_ref[2] ^ j) * part, part)
        piece[...] = out_ref[pl.ds(start, part), :]


def mixed_kernel(dims, *refs):
    per_expert, local = dims
    rets = refs[:local]
    x1_ref, prob_ref, ids_ref, slot_ref, out_ref = refs[local:]
    _, _, gates = pick_probs(ids_ref[...], prob_ref[...])
    out = x1_ref[...]
    for j in range(2):
        col = slot_ref[:, j : j + 1]
        y = mm(place_one(col, 0, per_expert), rets[0][...])
        for k in range(1, local):
            y += mm(place_one(col, k, per_expert), rets[k][...])
        out += gates[j] * y
    out_ref[...] = out.astype(BF16)


def last_kernel(dims, meta_ref, *refs):
    half, seqs, groups = dims
    parts = refs[:half]
    x_ref, dx1_ref, gain_ref, out_ref, acc_ref = refs[half:]
    z = meta_ref[0]
    rows = parts[0].shape[0]
    acc_ref[...] = jnp.zeros_like(acc_ref)
    for k in range(half):
        m = (2 * (z ^ k)) // groups
        acc_ref[m] += parts[k][...].astype(F32)
    gain = gain_ref[...]
    for m in range(seqs):
        part = slice(m * rows, (m + 1) * rows)
        x = x_ref[part, :].astype(F32)
        r = lax.rsqrt(jnp.mean(x * x, axis=1, keepdims=True) + EPS)
        u = x * r
        scaled = acc_ref[m] * gain
        back = r * (scaled - u * jnp.mean(u * scaled, axis=1, keepdims=True))
        out_ref[part, :] = (dx1_ref[part, :] + back).astype(BF16)


DP = ("hi", "lo")


def permute_xor(value, axis, offset):
    axis = DP if axis == "dp" else axis
    count = lax.axis_size(axis)
    return lax.ppermute(value, axis, [(i, i ^ offset) for i in range(count)])


def spread_dp(value):
    return [value] + [permute_xor(value, "dp", j) for j in range(1, lax.axis_size(DP))]


def swap_seq(value):
    return lax.all_to_all(value, "seq", split_axis=0, concat_axis=0, tiled=True)


def shards(
    tokens,
    cotangent,
    expert_ids,
    buckets,
    gain_attn,
    w_qkv,
    rel_bias,
    w_attn_out,
    gain_moe,
    router,
    w_up,
    w_down,
):
    micro, batch, rows, width = tokens.shape
    heads = width // HD
    seqs = micro * batch
    seq, dp = lax.axis_size("seq"), lax.axis_size(DP)
    half = seq // 2
    length = seq * rows
    groups = seq // seqs
    hpd = -(-heads // groups)
    width_h = hpd * HD
    padded_heads = hpd * groups
    total = seqs * rows
    experts, local = router.shape[1], w_up.shape[0]
    slots = seqs * (expert_ids.shape[3] * rows // experts + 2)
    cp = -(-(slots + 2) // 8) * 8
    per_expert = seq * cp
    block = 256
    scale = 1.0 / math.sqrt(HD)
    shard = w_qkv.shape[0]
    me, dpi = lax.axis_index("seq"), lax.axis_index(DP)
    z, c = me // 2, me % 2
    low = dp // 2
    my_group = me % groups
    meta = jnp.stack([z, c, dpi, dpi // low, my_group]).astype(jnp.int32)

    x_flat = tokens.reshape(seqs, rows, width)
    cot_flat = cotangent.reshape(total, width)
    ids_flat = expert_ids.reshape(total, expert_ids.shape[3])

    own, sib = [], []
    for k in range(half):
        target = (2 * (z ^ k)) // groups
        piece = lax.dynamic_index_in_dim(x_flat, target, 0, keepdims=False)
        if k:
            piece = permute_xor(piece, "seq", 2 * k)
        own.append(piece)
        sib.append(permute_xor(piece, "seq", 1))

    gain_lane = (3 * width_h) % LANES
    cols = max(3 * width_h - gain_lane + LANES, 3 * LANES)
    w_four = w_qkv.reshape(shard, 3, heads, HD)
    w_four = jnp.pad(w_four, ((0, 0), (0, 0), (0, padded_heads - heads), (0, 0)))
    w_groups = jnp.transpose(w_four.reshape(shard, 3, groups, width_h), (2, 0, 1, 3))
    w_groups = w_groups.reshape(groups, shard, 3 * width_h)
    gain_col = jnp.broadcast_to(gain_attn[None, :, None], (groups, shard, 1))
    w_groups = jnp.concatenate([w_groups, gain_col], axis=2)
    w_groups = jnp.pad(w_groups, ((0, 0), (0, 0), (0, cols - 3 * width_h - 1)))

    w_small = jnp.concatenate([w_attn_out, router, gain_moe[:, None]], axis=1)
    small_cols = -(-w_small.shape[1] // LANES) * LANES
    w_small = jnp.pad(w_small, ((0, 0), (0, small_cols - w_small.shape[1])))
    w_small = lax.all_gather(w_small, DP + ("seq",), axis=0, tiled=True)
    w_line = swap_seq(jnp.tile(w_groups, (seqs, 1, 1))).reshape(seq * shard, cols)
    w_parts = spread_dp(w_line)

    hot = (buckets[:, None] == jnp.arange(rel_bias.shape[0], dtype=jnp.int32)).astype(F32)
    repeat = LANES // rel_bias.shape[0]
    hot_rev = jnp.pad(jnp.tile(jnp.flip(hot, axis=0), (1, repeat)), ((0, block), (0, 0)))
    hot_rev = hot_rev.astype(BF16)
    table = jnp.pad(rel_bias.astype(F32), ((0, 0), (0, padded_heads - heads)))
    table = lax.dynamic_slice_in_dim(table, my_group * hpd, hpd, 1)
    by_distance = jnp.einsum("tn,nh->ht", hot, table, precision=lax.Precision.HIGHEST)
    bias_rev = jnp.concatenate(
        [jnp.flip(by_distance, axis=1), jnp.full((hpd, block), NEG, F32)], axis=1
    )

    slot_cols, cot_send = call(
        functools.partial(route_kernel, (total, experts, local, seq, cp)),
        [
            ((total, LANES), jnp.int32),
            ((2 * per_expert, width), BF16),
        ],
        [meta, ids_flat, cot_flat],
        smem=1,
        name="route",
        after=own[1:] + sib + w_parts,
    )

    def to_experts(value):
        got = swap_seq(value.reshape(seq, 2 * cp, width)).reshape(seq, 2, cp, width)
        first, second = (got[:, k].reshape(per_expert, width) for k in range(2))
        second = permute_xor(second, "dp", low)
        return [
            [item] + [permute_xor(item, "dp", j) for j in range(1, low)]
            for item in (first, second)
        ]

    cot_parts = to_experts(cot_send)
    ff = w_up.shape[2]
    away = 1 - dpi // low
    away_pair = jnp.stack(
        [lax.dynamic_index_in_dim(item, away, 0, keepdims=False) for item in (w_up, w_down)]
    )
    away_pair = lax.all_gather(away_pair, "hi", axis=0)
    away_got = lax.dynamic_index_in_dim(away_pair, away, 0, keepdims=False)
    up_got, down_got = away_got[0], away_got[1]
    up_own, down_own = (
        lax.dynamic_index_in_dim(item, 1 - away, 0, keepdims=False) for item in (w_up, w_down)
    )

    def from_experts(pieces):
        return [pieces[0]] + [permute_xor(pieces[j], "dp", j) for j in range(1, low)]

    o_all, qkv, xn1, w_mine, lse, slab, gain_first = call(
        functools.partial(attn_fwd_kernel, (half, dp, hpd, block, gain_lane, scale)),
        [
            ((length, width_h), BF16),
            ((length, cols), BF16),
            ((length, width), BF16),
            ((width, cols), BF16),
            ((length, LANES), F32),
            ((hpd, block, length), F32),
            ((1, width), F32),
        ],
        [meta] + own + sib + w_parts + [bias_rev],
        smem=1,
        name="attn_fwd",
        after=[cot_send, hot_rev],
    )
    o_mine = swap_seq(o_all.reshape(seq, rows, width_h))
    x1, xn2, probs, gain_second, send = call(
        functools.partial(mid_kernel, (seqs, groups, cp, slots, per_expert, experts)),
        [
            ((total, width), F32),
            ((total, width), BF16),
            ((total, experts), F32),
            ((1, width), F32),
        ]
        + [((2 * per_expert, width), BF16)],
        [o_mine, x_flat.reshape(total, width), ids_flat, slot_cols, w_small],
        name="mid",
        after=cot_parts[0],
    )

    slot_parts = to_experts(send)
    dx_sent, saved = [[], []], []
    for i in range(2):
        for j in range(low):
            dx_part, *rest = call(
                functools.partial(expert_kernel, (1, cp, slots)),
                [((per_expert, width), BF16)]
                + [((per_expert, ff), BF16)] * 4
                + [((per_expert, width), BF16)],
                [slot_parts[i][j], cot_parts[i][j], up_own, down_own, up_got, down_got],
                name="expert",
            )
            dx_sent[i].append(dx_part)
            saved.append(rest)
    grad_down, grad_down_away = call(
        functools.partial(down_grad_kernel, 2 * low),
        [((width, ff), F32), ((width, ff), BF16)],
        [item for one in saved for item in (one[0], one[1], one[4])],
        name="down_grad",
    )
    grad_down_pair = lax.all_gather(grad_down_away, "hi", axis=0)
    dx_sum = []
    for i in range(2):
        dx_sum += call(
            functools.partial(add_kernel, (cp, slots)),
            [((per_expert, width), BF16)],
            from_experts(dx_sent[i]),
            name="add_dx",
            after=[grad_down_away] if i else [],
        )
    y_sent = call(
        functools.partial(expert_out_kernel, (2 * low, 1)),
        [((per_expert, width), BF16)] * (2 * low),
        [item for one in saved for item in one[:2]] + [down_own, down_got],
        name="expert_out",
        after=[dx_sum[1]],
    )
    dx_swapped = permute_xor(dx_sum[1], "dp", low)
    ret_dx = [
        swap_seq(item.reshape(seq, cp, width)).reshape(per_expert, width)
        for item in (dx_sum[0], dx_swapped)
    ]
    y_back = [from_experts(y_sent[:low]), from_experts(y_sent[low:])]

    dx1, da, do_send, dlogits, prod = call(
        functools.partial(back_kernel, (seqs, groups, cp, slots, per_expert, local)),
        [
            ((total, width), F32),
            ((total, width), BF16),
            ((seq, rows, width_h), BF16),
            ((total, experts), F32),
            ((total, width), BF16),
        ],
        ret_dx
        + [x1, probs, ids_flat, slot_cols, cot_flat, w_small, gain_second],
        name="back",
        after=[y_sent[0]],
    )
    do_all = swap_seq(do_send).reshape(length, width_h)

    small_sent = call(
        functools.partial(small_grad_kernel, (seqs, groups)),
        [((width // dp, small_cols), BF16)] * dp,
        [meta, o_mine, da, xn2, dlogits, prod],
        scratch=[pltpu.VMEM((width, small_cols), BF16)],
        smem=1,
        name="small_grad",
    )
    small_got = [permute_xor(small_sent[j], "dp", j) if j else small_sent[j] for j in range(dp)]
    y_first, y_second = call(
        functools.partial(add_both_kernel, None),
        [((per_expert, width), BF16)] * 2,
        y_back[0] + y_back[1],
        name="add_y",
        after=[small_sent[0]],
    )

    y_swapped = permute_xor(y_second, "dp", low)
    (grad_up_away,) = call(
        functools.partial(up_grad_kernel, (2 * low, 1)),
        [((width, ff), BF16)],
        sum(slot_parts, []) + [one[3] for one in saved],
        name="up_grad_away",
        after=[y_swapped],
    )
    grad_up_pair = lax.all_gather(grad_up_away, "hi", axis=0)
    (y_pair,) = call(
        functools.partial(side_kernel, None),
        [((seq, 2 * cp, width), BF16)],
        [item.reshape(seq, cp, width) for item in (y_first, y_swapped)],
        name="side",
    )
    y_got = swap_seq(y_pair).reshape(seq, 2, cp, width)
    mixed_in = [y_got[:, k].reshape(per_expert, width) for k in range(2)]
    (mixed,) = call(
        functools.partial(mixed_kernel, (per_expert, local)),
        [((total, width), BF16)],
        mixed_in + [x1, probs, ids_flat, slot_cols],
        name="mixed",
    )


    span = length + block
    dx_own, dx_sib, dqkv, table_own = call(
        functools.partial(attn_bwd_kernel, (half, hpd, block, scale, rel_bias.shape[0])),
        [
            ((half, rows, width), BF16),
            ((half, rows, width), BF16),
            ((length, cols), BF16),
            ((8, LANES), F32),
        ],
        [meta, do_all, qkv, w_mine, lse, slab, hot_rev],
        scratch=[
            pltpu.VMEM((length, HD), F32),
            pltpu.VMEM((length, HD), F32),
            pltpu.VMEM((block, span), F32),
            pltpu.VMEM((8, span), F32),
        ],
        smem=1,
        name="attn_bwd",
        after=[y_pair, grad_up_away, small_sent[0]],
    )
    pairs = call(
        functools.partial(pair_kernel, None),
        [((rows, width), BF16)] * half,
        [dx_own, permute_xor(dx_sib, "seq", 1)],
        name="pair",
    )
    dx_parts = [permute_xor(pairs[k], "seq", 2 * k) if k else pairs[k] for k in range(half)]
    (grad_tokens,) = call(
        functools.partial(last_kernel, (half, seqs, groups)),
        [((total, width), BF16)],
        [meta] + dx_parts + [x_flat.reshape(total, width), dx1, gain_first],
        scratch=[pltpu.VMEM((seqs, rows, width), F32)],
        smem=1,
        name="last",
    )

    (grad_up,) = call(
        functools.partial(up_grad_kernel, (2 * low, 1)),
        [((width, ff), F32)],
        sum(slot_parts, []) + [one[2] for one in saved],
        name="up_grad",
        after=[pairs[0]],
    )
    cols_sent = call(
        functools.partial(cols_kernel, None),
        [((width // dp + 16, cols), BF16)] * dp,
        [meta, xn1, dqkv, table_own],
        scratch=[pltpu.VMEM((width, cols), BF16)],
        smem=1,
        name="cols",
        after=[pairs[0]],
    )
    cols_got = [permute_xor(cols_sent[j], "dp", j) if j else cols_sent[j] for j in range(dp)]
    line_rows = -(-shard // 8) * 8 + 8
    (line,) = call(
        functools.partial(merge_kernel, (dp, shard)),
        [((seq, line_rows, cols + small_cols), BF16)],
        cols_got + small_got,
        scratch=[pltpu.VMEM((width // dp, cols + small_cols), F32)],
        name="merge",
        after=dx_parts[1:],
    )
    both_up, both_down = call(
        functools.partial(both_experts_kernel, None),
        [((local, width, ff), F32)] * 2,
        [meta, grad_up, grad_up_pair, grad_down, grad_down_pair],
        smem=1,
        name="both_experts",
    )
    grad_qkv, grad_out, grad_router, grad_first, grad_second, table = call(
        functools.partial(finish_kernel, (seqs, groups, hpd, cols, experts)),
        [
            ((shard, 3 * width), F32),
            ((shard, width), F32),
            ((shard, experts), F32),
            ((1, shard), F32),
            ((1, shard), F32),
            ((8, LANES), F32),
        ],
        [swap_seq(line), w_qkv, gain_attn[:, None]],
        name="finish",
        after=[grad_tokens, mixed, both_up],
    )
    table = table.reshape(8, repeat, rel_bias.shape[0])
    table = jnp.transpose(table, (2, 1, 0)).reshape(rel_bias.shape[0], 8 * repeat)
    table_grad = table[:, :heads]

    return (
        mixed.reshape(tokens.shape),
        grad_tokens.reshape(tokens.shape),
        grad_first.reshape(shard),
        grad_qkv,
        table_grad,
        grad_out,
        grad_second.reshape(shard),
        grad_router,
        both_up,
        both_down,
    )


def solution(mesh):
    dp, seq = mesh.devices.shape
    mesh = Mesh(mesh.devices.reshape(2, dp // 2, seq), DP + ("seq",))
    in_specs = (
        P(None, DP, "seq", None),
        P(None, DP, "seq", None),
        P(None, DP, "seq", None),
        P(),
        P(("hi", "lo", "seq")),
        P(("hi", "lo", "seq"), None),
        P(),
        P(("hi", "lo", "seq"), None),
        P(("hi", "lo", "seq")),
        P(("hi", "lo", "seq"), None),
        P("seq", None, DP),
        P("seq", None, DP),
    )
    out_specs = (
        P(None, DP, "seq", None),
        P(None, DP, "seq", None),
        P(("hi", "lo", "seq")),
        P(("hi", "lo", "seq"), None),
        P(),
        P(("hi", "lo", "seq"), None),
        P(("hi", "lo", "seq")),
        P(("hi", "lo", "seq"), None),
        P("seq", None, DP),
        P("seq", None, DP),
    )
    return jax.shard_map(shards, mesh=mesh, in_specs=in_specs, out_specs=out_specs, check_vma=False)
```

```python
import functools
import math

import jax
import jax.numpy as jnp
from jax import lax
from jax.experimental import pallas as pl
from jax.experimental.pallas import tpu as pltpu
from jax.sharding import Mesh
from jax.sharding import PartitionSpec as P

HD = 64
LANES = 128
EPS = 1e-06
NEG = -1e30
F32 = jnp.float32
BF16 = jnp.bfloat16
VMEM_BYTES = 56 * 1024 * 1024
INV_SQRT2 = 1.0 / math.sqrt(2.0)
INV_SQRT2PI = 1.0 / math.sqrt(2.0 * math.pi)


def mm(a, b):
    return lax.dot_general(a, b, (((1,), (0,)), ((), ())), preferred_element_type=F32)


def mm_nt(a, b):
    return lax.dot_general(a, b, (((1,), (1,)), ((), ())), preferred_element_type=F32)


def mm_tn(a, b):
    return lax.dot_general(a, b, (((0,), (0,)), ((), ())), preferred_element_type=F32)


def iota(shape, dim):
    return lax.broadcasted_iota(jnp.int32, shape, dim)


def split3(v):
    hi = v.astype(BF16).astype(F32)
    rest = v - hi
    mid = rest.astype(BF16).astype(F32)
    return hi, mid, rest - mid


def call(kernel, outs, ins, scratch=(), smem=0, name=None, after=()):
    spec = [pl.BlockSpec(memory_space=pltpu.SMEM)] * smem
    spec += [pl.BlockSpec(memory_space=pltpu.VMEM)] * (len(ins) - smem)
    spec += [pl.BlockSpec(memory_space=pl.ANY)] * len(after)
    count = len(ins)

    def body(*refs):
        kernel(*refs[:count], *refs[count + len(after) :])

    return pl.pallas_call(
        body,
        out_shape=[jax.ShapeDtypeStruct(s, d) for s, d in outs],
        in_specs=spec,
        out_specs=[pl.BlockSpec(memory_space=pltpu.VMEM)] * len(outs),
        scratch_shapes=list(scratch),
        compiler_params=pltpu.CompilerParams(vmem_limit_bytes=VMEM_BYTES),
        cost_estimate=pl.CostEstimate(flops=0, transcendentals=0, bytes_accessed=1),
        name=name,
    )(*ins, *after)


def route_kernel(dims, meta_ref, ids_ref, cot_ref, slot_ref, out_ref):
    rows, experts, local, seq, cp = dims
    ids = ids_ref[...]
    expert = iota((rows, experts), 1)
    hot = [(ids[:, j : j + 1] == expert).astype(F32) for j in range(2)]
    before = (iota((rows, rows), 0) > iota((rows, rows), 1)).astype(BF16)
    rank = mm(before, (hot[0] + hot[1]).astype(BF16))
    cols = []
    for j in range(2):
        own = jnp.sum(hot[j] * rank, axis=1, keepdims=True).astype(jnp.int32)
        e = ids[:, j : j + 1]
        cols.append(((e % local) ^ meta_ref[3]) * (seq * cp) + (e // local) * cp + own)
    lane = iota((rows, LANES), 1)
    slot_ref[...] = jnp.where(lane == 0, cols[0], cols[1])
    place = place_both([merged(col, cp, seq * cp) for col in cols], 0, 2 * seq * cp)
    out_ref[...] = mm_tn(place, cot_ref[...]).astype(BF16)


def merged(col, cp, per_expert):
    inside = col % per_expert
    return inside // cp * (2 * cp) + col // per_expert * cp + inside % cp


def place_one(col, e, count):
    return (iota((col.shape[0], count), 1) + e * count == col).astype(BF16)


def place_both(cols, e, count):
    where = iota((cols[0].shape[0], count), 1) + e * count
    return jnp.logical_or(where == cols[0], where == cols[1]).astype(BF16)


def attn_fwd_kernel(dims, meta_ref, *refs):
    half, dp, hpd, block, gain_lane, scale = dims
    own, sib, wp = refs[:half], refs[half : 2 * half], refs[2 * half : 2 * half + dp]
    brev_ref = refs[2 * half + dp]
    o_ref, qkv_ref, xn_ref, w_ref, lse_ref, slab_ref, gain_ref = refs[2 * half + dp + 1 :]
    z, c, d = meta_ref[0], meta_ref[1], meta_ref[2]
    part = wp[0].shape[0]
    for j in range(dp):
        w_ref[pl.ds(pl.multiple_of((d ^ j) * part, part), part), :] = wp[j][...]
    tile = 3 * hpd * HD // LANES * LANES
    turned = jnp.transpose(w_ref[:, tile : tile + LANES].astype(F32))
    gain = turned[gain_lane : gain_lane + 1, :]
    gain_ref[...] = gain
    rows = own[0].shape[0]
    for group, core in ((own, c), (sib, 1 - c)):
        for k in range(half):
            x = group[k][...].astype(F32)
            r = lax.rsqrt(jnp.mean(x * x, axis=1, keepdims=True) + EPS)
            start = pl.multiple_of((2 * (z ^ k) + core) * rows, rows)
            xn_ref[pl.ds(start, rows), :] = (x * r * gain).astype(BF16)
    length = xn_ref.shape[0]
    for i in range(length // block):
        part_rows = slice(i * block, (i + 1) * block)
        qkv_ref[part_rows, :] = mm(xn_ref[part_rows, :], w_ref[...]).astype(BF16)
    span = length + block
    width_h = hpd * HD
    for h in range(hpd):
        base = brev_ref[h : h + 1, :]
        rolled = [base if i == 7 else pltpu.roll(base, span - (7 - i), 1) for i in range(8)]
        slab = jnp.concatenate(rolled, axis=0)
        n = 8
        while n < block:
            slab = jnp.concatenate([pltpu.roll(slab, span - n, 1), slab], axis=0)
            n *= 2
        slab_ref[h] = slab[:, :length]
    lane = iota((block, LANES), 1)
    for i in range(length // block):
        q_rows = slice(i * block, (i + 1) * block)
        keys = (i + 1) * block
        lse = jnp.zeros((block, LANES), F32)
        for h in range(hpd):
            q = qkv_ref[q_rows, h * HD : (h + 1) * HD] * jnp.asarray(scale, BF16)
            k = qkv_ref[:keys, width_h + h * HD : width_h + (h + 1) * HD]
            v = qkv_ref[:keys, 2 * width_h + h * HD : 2 * width_h + (h + 1) * HD]
            s = mm_nt(q, k) + slab_ref[h, :, length - keys :]
            top = jnp.max(s, axis=1, keepdims=True)
            e = jnp.exp(s - top)
            total = jnp.sum(e, axis=1, keepdims=True)
            p = (e * (1.0 / total)).astype(BF16)
            o_ref[q_rows, h * HD : (h + 1) * HD] = mm(p, v).astype(BF16)
            lse = jnp.where(lane == h, top + jnp.log(total), lse)
        lse_ref[q_rows, :] = lse


def three_parts(table, width):
    wide = jnp.concatenate(list(split3(table)), axis=1)
    if width > 3 * LANES:
        wide = jnp.concatenate([wide, jnp.zeros((8, width - 3 * LANES), F32)], axis=1)
    return jnp.concatenate([wide, jnp.zeros_like(wide)], axis=0).astype(BF16)


def attn_bwd_kernel(dims, meta_ref, do_ref, qkv_ref, w_ref, lse_ref, slab_ref, *refs):
    half, hpd, block, scale, buckets = dims
    hot_ref, dx_own, dx_sib, dqkv_ref, table_ref, dk_ref, dv_ref, db_ref, gb_ref = refs
    gb_ref[...] = jnp.zeros_like(gb_ref)
    z, c = meta_ref[0], meta_ref[1]
    length = qkv_ref.shape[0]
    width_h = hpd * HD
    blocks = length // block
    dqkv_ref[...] = jnp.zeros_like(dqkv_ref)
    for h in range(hpd):
        cols = slice(h * HD, (h + 1) * HD)
        k_cols = slice(width_h + h * HD, width_h + (h + 1) * HD)
        v_cols = slice(2 * width_h + h * HD, 2 * width_h + (h + 1) * HD)
        for i in range(blocks - 1, -1, -1):
            rows = slice(i * block, (i + 1) * block)
            keys = (i + 1) * block
            q = qkv_ref[rows, cols] * jnp.asarray(scale, BF16)
            k = qkv_ref[:keys, k_cols]
            v = qkv_ref[:keys, v_cols]
            do = do_ref[rows, cols]
            s = mm_nt(q, k) + slab_ref[h, :, length - keys :]
            p = jnp.exp(s - lse_ref[rows, h : h + 1])
            dprob = mm_nt(do, v)
            delta = jnp.sum(p * dprob, axis=1, keepdims=True)
            ds32 = p * (dprob - delta)
            ds = ds32.astype(BF16)
            dqkv_ref[rows, cols] = (mm(ds, k) * scale).astype(BF16)
            dk = mm_tn(ds, q)
            dv = mm_tn(p.astype(BF16), do)
            if i == blocks - 1:
                dk_ref[...] = dk
                dv_ref[...] = dv
                db_ref[:, :length] = ds.astype(F32)
            else:
                dk_ref[:keys, :] += dk
                dv_ref[:keys, :] += dv
                db_ref[:, length - keys : length] += ds.astype(F32)
        dqkv_ref[:, k_cols] = dk_ref[...].astype(BF16)
        dqkv_ref[:, v_cols] = dv_ref[...].astype(BF16)
        db_ref[:, length:] = jnp.zeros((block, block), F32)
        n = block
        acc = db_ref[...]
        while n > 1:
            n //= 2
            acc = pltpu.roll(acc[:n], n, 1) + acc[n:]
        gb_ref[h : h + 1, :] = acc
    hot = hot_ref[...]
    hi, mid, low = split3(gb_ref[...])
    by_bucket = mm(hi.astype(BF16), hot) + mm(mid.astype(BF16), hot) + mm(low.astype(BF16), hot)
    table = jnp.zeros((8, LANES), F32)
    row, lane = iota((8, LANES), 0), iota((8, LANES), 1)
    for h in range(hpd):
        head = meta_ref[4] * hpd + h
        here = jnp.logical_and(row == head % 8, lane // buckets == head // 8)
        table = jnp.where(here, by_bucket[h : h + 1, :], table)
    table_ref[...] = table
    rows = dx_own.shape[1]
    w = w_ref[...]
    for out_ref, core in ((dx_own, c), (dx_sib, 1 - c)):
        for k in range(half):
            start = pl.multiple_of((2 * (z ^ k) + core) * rows, rows)
            out_ref[k] = mm_nt(dqkv_ref[pl.ds(start, rows), :], w).astype(BF16)


def cols_kernel(dims, meta_ref, xn_ref, dqkv_ref, table_ref, *refs):
    gq_refs, gq_ref = refs[:-1], refs[-1]
    gq_ref[...] = mm_tn(xn_ref[...], dqkv_ref[...]).astype(BF16)
    table = three_parts(table_ref[...], gq_ref.shape[1])
    part = gq_refs[0].shape[0] - 16
    for j, piece in enumerate(gq_refs):
        start = pl.multiple_of((meta_ref[2] ^ j) * part, part)
        piece[:part, :] = gq_ref[pl.ds(start, part), :]
        piece[part:, :] = table


def pick_probs(ids, probs):
    expert = iota(probs.shape, 1)
    hot = [(ids[:, j : j + 1] == expert).astype(F32) for j in range(2)]
    picked = [jnp.sum(probs * one, axis=1, keepdims=True) for one in hot]
    total = picked[0] + picked[1]
    return hot, total, [one / total for one in picked]


def norm_parts(x1):
    r = lax.rsqrt(jnp.mean(x1 * x1, axis=1, keepdims=True) + EPS)
    return r, x1 * r


def head_rows(groups, width_h, width):
    return [(g, min(width_h, width - g * width_h)) for g in range(groups) if g * width_h < width]


def mid_kernel(dims, o_ref, x_ref, ids_ref, slot_ref, *refs):
    seqs, groups, cp, dead, per_expert, experts = dims
    ws_ref, x1_ref, xn_ref, prob_ref, gain_ref, send_ref = refs
    width = x_ref.shape[1]
    lane_at = width + experts
    tile = lane_at // LANES * LANES
    turned = jnp.transpose(ws_ref[:, tile : tile + LANES].astype(F32))
    gain = turned[lane_at - tile : lane_at - tile + 1, :]
    gain_ref[...] = gain
    rows = x_ref.shape[0] // seqs
    width_h = o_ref.shape[2]
    for m in range(seqs):
        part = slice(m * rows, (m + 1) * rows)
        acc = x_ref[part, :].astype(F32)
        for g, count in head_rows(groups, width_h, width):
            w_rows = ws_ref[g * width_h : g * width_h + count, :width]
            acc += mm(o_ref[m * groups + g][:, :count], w_rows)
        x1_ref[part, :] = acc
    r, u = norm_parts(x1_ref[...])
    xn = (u * gain).astype(BF16)
    xn_ref[...] = xn
    logits = mm(xn, ws_ref[:, width : width + experts])
    e = jnp.exp(logits - jnp.max(logits, axis=1, keepdims=True))
    probs = e / jnp.sum(e, axis=1, keepdims=True)
    prob_ref[...] = probs
    ids = ids_ref[...]
    _, _, gates = pick_probs(ids, probs)
    cols = [slot_ref[:, j : j + 1] for j in range(2)]
    lane = iota((xn.shape[0], LANES), 1)
    places = [merged(col, cp, per_expert) for col in cols]
    out = mm_tn(place_both(places, 0, 2 * per_expert), xn)
    extra = jnp.zeros((2 * per_expert, LANES), F32)
    for j in range(2):
        rank = cols[j] % cp
        hi, mid, low = split3(gates[j])
        value = jnp.where(lane < cp, hi, jnp.where(lane < 2 * cp, mid, low))
        keep = jnp.logical_and(lane % cp == rank, lane < 3 * cp)
        carried = jnp.where(keep, value, 0.0).astype(BF16)
        extra += mm_tn(place_one(places[j] - rank + dead, 0, 2 * per_expert), carried)
    send_ref[:, LANES:] = out[:, LANES:].astype(BF16)
    send_ref[:, :LANES] = (out[:, :LANES] + extra).astype(BF16)


def expert_kernel(dims, *refs):
    count, cp, dead = dims
    xs, cs = refs[:count], refs[count : 2 * count]
    weights = refs[2 * count : 2 * count + 4]
    outs = refs[2 * count + 4 :]
    dx_refs = outs[:count]
    h_refs, dpre_refs, dy_ref = outs[count : count + 2], outs[count + 2 : count + 4], outs[count + 4]
    rows = xs[0].shape[0]
    chunks = rows // cp
    lane = iota((rows, LANES), 1)
    row = iota((rows, LANES), 0)
    take = (iota((chunks, rows), 1) == iota((chunks, rows), 0) * cp + dead).astype(BF16)
    spread = (iota((rows, chunks), 0) // cp == iota((rows, chunks), 1)).astype(BF16)
    mine = jnp.logical_and(lane % cp == row % cp, lane < 3 * cp)
    mine_first = lane == row % cp
    target = iota((rows, rows), 1) // cp * cp + dead
    put_hi = (iota((rows, rows), 0) == target).astype(BF16)
    put_low = (iota((rows, rows), 0) == target + 1).astype(BF16)
    for j in range(count):
        part = slice(j * rows, (j + 1) * rows)
        x = xs[j][...]
        cot = cs[j][...]
        carried = mm(spread, mm(take, x[:, :LANES]).astype(BF16))
        gate = jnp.sum(jnp.where(mine, carried, 0.0), axis=1, keepdims=True)
        dy_ref[part, :] = (cot.astype(F32) * gate).astype(BF16)
        dg = jnp.zeros((rows, 1), F32)
        dx = jnp.zeros((rows, x.shape[1]), F32)
        for f in range(2):
            pre = mm(x, weights[2 * f][...])
            cdf = 0.5 * (1.0 + lax.erf(pre * INV_SQRT2))
            hidden = pre * cdf
            h_refs[f][part, :] = hidden.astype(BF16)
            slope = cdf + pre * (jnp.exp(-0.5 * pre * pre) * INV_SQRT2PI)
            dh = mm(cot, weights[2 * f + 1][...])
            dg += jnp.sum(hidden * dh, axis=1, keepdims=True)
            dpre = (dh * slope * gate).astype(BF16)
            dpre_refs[f][part, :] = dpre
            dx += mm_nt(dpre, weights[2 * f][...])
        dg_hi = dg.astype(BF16).astype(F32)
        extra = mm(put_hi, jnp.where(mine_first, dg_hi, 0.0).astype(BF16))
        extra += mm(put_low, jnp.where(mine_first, dg - dg_hi, 0.0).astype(BF16))
        dx_refs[j][:, LANES:] = dx[:, LANES:].astype(BF16)
        dx_refs[j][:, :LANES] = (dx[:, :LANES] + extra).astype(BF16)


def up_grad_kernel(dims, *refs):
    calls, count = dims
    xs, dpre, out_ref = refs[: calls * count], refs[calls * count : -1], refs[-1]
    rows = xs[0].shape[0]
    acc = None
    for i in range(calls):
        for j in range(count):
            term = mm_tn(xs[i * count + j][...], dpre[i][j * rows : (j + 1) * rows, :])
            acc = term if acc is None else acc + term
    out_ref[...] = acc.astype(out_ref.dtype)


def expert_out_kernel(dims, *refs):
    calls, count = dims
    hidden, weights, outs = refs[: 2 * calls], refs[2 * calls : 2 * calls + 2], refs[2 * calls + 2 :]
    rows = outs[0].shape[0]
    for i in range(calls):
        for j in range(count):
            part = slice(j * rows, (j + 1) * rows)
            y = mm_nt(hidden[2 * i][part, :], weights[0][...])
            y += mm_nt(hidden[2 * i + 1][part, :], weights[1][...])
            outs[i * count + j][...] = y.astype(BF16)


def down_grad_kernel(dims, *refs):
    calls = dims
    saved, outs = refs[: 3 * calls], refs[3 * calls :]
    for f in range(2):
        acc = mm_tn(saved[2][...], saved[f][...])
        for i in range(1, calls):
            acc += mm_tn(saved[3 * i + 2][...], saved[3 * i + f][...])
        outs[f][...] = acc.astype(outs[f].dtype)


def both_experts_kernel(dims, meta_ref, up_ref, up_pair, down_ref, down_pair, out_up, out_down):
    bit = meta_ref[3]
    for own, pair, out in ((up_ref, up_pair, out_up), (down_ref, down_pair, out_down)):
        out[bit] = own[...]
        out[1 - bit] = pair[1 - bit].astype(F32)


def merge_kernel(dims, *refs):
    dp, shard = dims
    lines, smalls, out_ref, acc_ref = refs[:dp], refs[dp : 2 * dp], refs[2 * dp], refs[2 * dp + 1]
    part = smalls[0].shape[0]
    cols = lines[0].shape[1]
    table = jnp.zeros((8, LANES), F32)
    acc = jnp.zeros((part, cols), F32)
    small = jnp.zeros(smalls[0].shape, F32)
    for j in range(dp):
        acc += lines[j][:part, :].astype(F32)
        tail = lines[j][part:, :].astype(F32)[:8]
        table += sum(tail[:, i * LANES : (i + 1) * LANES] for i in range(3))
        small += smalls[j][...].astype(F32)
    acc_ref[:, :cols] = acc
    acc_ref[:, cols:] = small
    width = acc_ref.shape[1]
    rows = out_ref.shape[1]
    tail = jnp.concatenate(list(split3(table)), axis=1)
    tail = jnp.concatenate([tail, jnp.zeros((8, width - 3 * LANES), F32)], axis=1)
    fill = rows - 8 - shard
    for s in range(out_ref.shape[0]):
        block = [acc_ref[s * shard : (s + 1) * shard, :], tail]
        if fill:
            block = [block[0], jnp.zeros((fill, width), F32), tail]
        out_ref[s] = jnp.concatenate(block, axis=0).astype(BF16)


def finish_kernel(dims, got_ref, w_ref, gain_ref, *outs):
    seqs, groups, hpd, cols, experts = dims
    qkv_ref, out_ref, router_ref, first_ref, second_ref, table_ref = outs
    width_h = hpd * HD
    shard, width = w_ref.shape[0], w_ref.shape[1] // 3
    got = [got_ref[s].astype(F32) for s in range(seqs * groups)]
    whole = functools.reduce(jnp.add, got)
    last = whole.shape[0] - 8
    table_ref[...] = sum(whole[last:, i * LANES : (i + 1) * LANES] for i in range(3))
    small = whole[:shard, cols:]
    out_ref[...] = small[:, :width]
    router_ref[...] = small[:, width : width + experts]
    tile = (width + experts) // LANES * LANES
    turned = jnp.transpose(pad_rows(small[:, tile : tile + LANES]))
    second_ref[...] = turned[width + experts - tile :][:1, :shard]
    for g, count in head_rows(groups, width_h, width):
        acc = functools.reduce(jnp.add, [got[m * groups + g][:shard, :cols] for m in range(seqs)])
        for i in range(3):
            start = i * width + g * width_h
            qkv_ref[:, start : start + count] = acc[:, i * width_h : i * width_h + count]
    total = jnp.sum(qkv_ref[...] * w_ref[...].astype(F32), axis=1, keepdims=True)
    total = jnp.broadcast_to(total / gain_ref[...].astype(F32), (shard, LANES))
    first_ref[...] = jnp.transpose(pad_rows(total))[:1, :shard]


def pad_rows(value):
    count = LANES - value.shape[0]
    return jnp.concatenate([value, jnp.zeros((count, value.shape[1]), F32)], axis=0)


def add_kernel(dims, *refs):
    cp, dead = dims
    parts, out_ref = refs[:-1], refs[-1]
    acc = parts[0][...].astype(F32)
    for part in parts[1:]:
        acc += part[...].astype(F32)
    if dead is None:
        out_ref[...] = acc.astype(BF16)
        return
    out_ref[:, LANES:] = acc[:, LANES:].astype(BF16)
    first = acc[:, :LANES]
    rows = first.shape[0]
    place = iota((rows, LANES), 0) % cp
    both = first + pltpu.roll(first, rows - 1, 0)
    high = both.astype(BF16).astype(F32)
    low = pltpu.roll(both - high, 1, 0)
    out = jnp.where(place == dead, high, jnp.where(place == dead + 1, low, first))
    out_ref[:, :LANES] = out.astype(BF16)


def add_both_kernel(dims, *refs):
    count = (len(refs) - 2) // 2
    for i in range(2):
        acc = refs[i * count][...].astype(F32)
        for part in refs[i * count + 1 : (i + 1) * count]:
            acc += part[...].astype(F32)
        refs[2 * count + i][...] = acc.astype(BF16)


def back_kernel(dims, *refs):
    seqs, groups, cp, dead, per_expert, local = dims
    rets = refs[:local]
    x1_ref, prob_ref, ids_ref, slot_ref, cot_ref = refs[local : local + 5]
    ws_ref, gain_ref = refs[local + 5 : local + 7]
    dx1_ref, da_ref, do_ref, dl_ref, prod_ref = refs[local + 7 :]
    width = x1_ref.shape[1]
    ids = ids_ref[...]
    probs = prob_ref[...]
    hot, total, gates = pick_probs(ids, probs)
    cols = [slot_ref[:, j : j + 1] for j in range(2)]
    rows = ids.shape[0]
    lane = iota((rows, LANES), 1)
    ranks = [col % cp for col in cols]
    moe = jnp.zeros(x1_ref.shape, F32)
    heads = [jnp.zeros((rows, LANES), F32) for _ in range(2)]
    for k in range(local):
        ret = rets[k][...]
        moe += mm(place_both(cols, k, per_expert), ret)
        for j in range(2):
            base = cols[j] - ranks[j] + dead
            heads[j] += mm(place_both([base, base + 1], k, per_expert), ret[:, :LANES])
    dg = [
        jnp.sum(jnp.where(lane == ranks[j], heads[j], 0.0), axis=1, keepdims=True) for j in range(2)
    ]
    mean_dg = dg[0] * gates[0] + dg[1] * gates[1]
    dprob = hot[0] * ((dg[0] - mean_dg) / total) + hot[1] * ((dg[1] - mean_dg) / total)
    dl = probs * (dprob - jnp.sum(probs * dprob, axis=1, keepdims=True))
    dl_ref[...] = dl
    router = ws_ref[:, width : width + probs.shape[1]]
    dl_hi = dl.astype(BF16)
    dl_low = (dl - dl_hi.astype(F32)).astype(BF16)
    dxn = moe + mm_nt(dl_hi, router) + mm_nt(dl_low, router)
    r, u = norm_parts(x1_ref[...])
    prod_ref[...] = (dxn * u).astype(BF16)
    scaled = dxn * gain_ref[...]
    dx1 = cot_ref[...].astype(F32) + r * (
        scaled - u * jnp.mean(u * scaled, axis=1, keepdims=True)
    )
    dx1_ref[...] = dx1
    da = dx1.astype(BF16)
    da_ref[...] = da
    width_h = do_ref.shape[2]
    each = rows // seqs
    used = head_rows(groups, width_h, width)
    if len(used) < groups or used[-1][1] < width_h:
        do_ref[...] = jnp.zeros_like(do_ref)
    for g, count in used:
        block = mm_nt(da, ws_ref[g * width_h : g * width_h + count, :width]).astype(BF16)
        for m in range(seqs):
            do_ref[m * groups + g, :, :count] = block[m * each : (m + 1) * each, :]


def side_kernel(dims, first_ref, second_ref, out_ref):
    both = [first_ref[...].astype(F32), second_ref[...].astype(F32)]
    out_ref[...] = jnp.concatenate(both, axis=1).astype(BF16)


def pair_kernel(dims, own_ref, got_ref, *outs):
    for k, out_ref in enumerate(outs):
        out_ref[...] = (own_ref[k].astype(F32) + got_ref[k].astype(F32)).astype(BF16)


def small_grad_kernel(dims, meta_ref, o_ref, da_ref, xn_ref, dl_ref, prod_ref, *refs):
    seqs, groups = dims
    pieces, out_ref = refs[:-1], refs[-1]
    width_h = o_ref.shape[2]
    rows, width = da_ref.shape
    each = rows // seqs
    experts = dl_ref.shape[1]
    for g, count in head_rows(groups, width_h, width):
        acc = jnp.zeros((width_h, width), F32)
        for m in range(seqs):
            acc += mm_tn(o_ref[m * groups + g], da_ref[m * each : (m + 1) * each, :])
        out_ref[g * width_h : g * width_h + count, :width] = acc[:count].astype(BF16)
    dl = dl_ref[...]
    dl_hi = dl.astype(BF16)
    dl_low = (dl - dl_hi.astype(F32)).astype(BF16)
    xn = xn_ref[...]
    tail = out_ref.shape[1] - width
    cut = (iota((experts, tail), 0) == iota((experts, tail), 1)).astype(BF16)
    router_part = mm_tn(xn, mm(dl_hi, cut).astype(BF16)) + mm_tn(xn, mm(dl_low, cut).astype(BF16))
    ones = (iota((rows, tail), 1) == experts).astype(BF16)
    out_ref[:, width:] = (router_part + mm_tn(prod_ref[...], ones)).astype(BF16)
    part = pieces[0].shape[0]
    for j, piece in enumerate(pieces):
        start = pl.multiple_of((meta_ref[2] ^ j) * part, part)
        piece[...] = out_ref[pl.ds(start, part), :]


def mixed_kernel(dims, *refs):
    per_expert, local = dims
    rets = refs[:local]
    x1_ref, prob_ref, ids_ref, slot_ref, out_ref = refs[local:]
    _, _, gates = pick_probs(ids_ref[...], prob_ref[...])
    out = x1_ref[...]
    for j in range(2):
        col = slot_ref[:, j : j + 1]
        y = mm(place_one(col, 0, per_expert), rets[0][...])
        for k in range(1, local):
            y += mm(place_one(col, k, per_expert), rets[k][...])
        out += gates[j] * y
    out_ref[...] = out.astype(BF16)


def last_kernel(dims, meta_ref, *refs):
    half, seqs, groups = dims
    parts = refs[:half]
    x_ref, dx1_ref, gain_ref, out_ref, acc_ref = refs[half:]
    z = meta_ref[0]
    rows = parts[0].shape[0]
    acc_ref[...] = jnp.zeros_like(acc_ref)
    for k in range(half):
        m = (2 * (z ^ k)) // groups
        acc_ref[m] += parts[k][...].astype(F32)
    gain = gain_ref[...]
    for m in range(seqs):
        part = slice(m * rows, (m + 1) * rows)
        x = x_ref[part, :].astype(F32)
        r = lax.rsqrt(jnp.mean(x * x, axis=1, keepdims=True) + EPS)
        u = x * r
        scaled = acc_ref[m] * gain
        back = r * (scaled - u * jnp.mean(u * scaled, axis=1, keepdims=True))
        out_ref[part, :] = (dx1_ref[part, :] + back).astype(BF16)


DP = ("hi", "lo")


def permute_xor(value, axis, offset):
    axis = DP if axis == "dp" else axis
    count = lax.axis_size(axis)
    return lax.ppermute(value, axis, [(i, i ^ offset) for i in range(count)])


def spread_dp(value):
    return [value] + [permute_xor(value, "dp", j) for j in range(1, lax.axis_size(DP))]


def swap_seq(value):
    return lax.all_to_all(value, "seq", split_axis=0, concat_axis=0, tiled=True)


def shards(
    tokens,
    cotangent,
    expert_ids,
    buckets,
    gain_attn,
    w_qkv,
    rel_bias,
    w_attn_out,
    gain_moe,
    router,
    w_up,
    w_down,
):
    micro, batch, rows, width = tokens.shape
    heads = width // HD
    seqs = micro * batch
    seq, dp = lax.axis_size("seq"), lax.axis_size(DP)
    half = seq // 2
    length = seq * rows
    groups = seq // seqs
    hpd = -(-heads // groups)
    width_h = hpd * HD
    padded_heads = hpd * groups
    total = seqs * rows
    experts, local = router.shape[1], w_up.shape[0]
    slots = seqs * (expert_ids.shape[3] * rows // experts + 2)
    cp = -(-(slots + 2) // 8) * 8
    per_expert = seq * cp
    block = 256
    scale = 1.0 / math.sqrt(HD)
    shard = w_qkv.shape[0]
    me, dpi = lax.axis_index("seq"), lax.axis_index(DP)
    z, c = me // 2, me % 2
    low = dp // 2
    my_group = me % groups
    meta = jnp.stack([z, c, dpi, dpi // low, my_group]).astype(jnp.int32)

    x_flat = tokens.reshape(seqs, rows, width)
    cot_flat = cotangent.reshape(total, width)
    ids_flat = expert_ids.reshape(total, expert_ids.shape[3])

    own, sib = [], []
    for k in range(half):
        target = (2 * (z ^ k)) // groups
        piece = lax.dynamic_index_in_dim(x_flat, target, 0, keepdims=False)
        if k:
            piece = permute_xor(piece, "seq", 2 * k)
        own.append(piece)
        sib.append(permute_xor(piece, "seq", 1))

    gain_lane = (3 * width_h) % LANES
    cols = max(3 * width_h - gain_lane + LANES, 3 * LANES)
    w_four = w_qkv.reshape(shard, 3, heads, HD)
    w_four = jnp.pad(w_four, ((0, 0), (0, 0), (0, padded_heads - heads), (0, 0)))
    w_groups = jnp.transpose(w_four.reshape(shard, 3, groups, width_h), (2, 0, 1, 3))
    w_groups = w_groups.reshape(groups, shard, 3 * width_h)
    gain_col = jnp.broadcast_to(gain_attn[None, :, None], (groups, shard, 1))
    w_groups = jnp.concatenate([w_groups, gain_col], axis=2)
    w_groups = jnp.pad(w_groups, ((0, 0), (0, 0), (0, cols - 3 * width_h - 1)))

    w_small = jnp.concatenate([w_attn_out, router, gain_moe[:, None]], axis=1)
    small_cols = -(-w_small.shape[1] // LANES) * LANES
    w_small = jnp.pad(w_small, ((0, 0), (0, small_cols - w_small.shape[1])))
    w_small = lax.all_gather(w_small, DP + ("seq",), axis=0, tiled=True)
    w_line = swap_seq(jnp.tile(w_groups, (seqs, 1, 1))).reshape(seq * shard, cols)
    w_parts = spread_dp(w_line)

    hot = (buckets[:, None] == jnp.arange(rel_bias.shape[0], dtype=jnp.int32)).astype(F32)
    repeat = LANES // rel_bias.shape[0]
    hot_rev = jnp.pad(jnp.tile(jnp.flip(hot, axis=0), (1, repeat)), ((0, block), (0, 0)))
    hot_rev = hot_rev.astype(BF16)
    table = jnp.pad(rel_bias.astype(F32), ((0, 0), (0, padded_heads - heads)))
    table = lax.dynamic_slice_in_dim(table, my_group * hpd, hpd, 1)
    by_distance = jnp.einsum("tn,nh->ht", hot, table, precision=lax.Precision.HIGHEST)
    bias_rev = jnp.concatenate(
        [jnp.flip(by_distance, axis=1), jnp.full((hpd, block), NEG, F32)], axis=1
    )

    slot_cols, cot_send = call(
        functools.partial(route_kernel, (total, experts, local, seq, cp)),
        [
            ((total, LANES), jnp.int32),
            ((2 * per_expert, width), BF16),
        ],
        [meta, ids_flat, cot_flat],
        smem=1,
        name="route",
        after=own[1:] + sib + w_parts,
    )

    def to_experts(value):
        got = swap_seq(value.reshape(seq, 2 * cp, width)).reshape(seq, 2, cp, width)
        first, second = (got[:, k].reshape(per_expert, width) for k in range(2))
        second = permute_xor(second, "dp", low)
        return [
            [item] + [permute_xor(item, "dp", j) for j in range(1, low)]
            for item in (first, second)
        ]

    cot_parts = to_experts(cot_send)
    ff = w_up.shape[2]
    away = 1 - dpi // low
    away_pair = jnp.stack(
        [lax.dynamic_index_in_dim(item, away, 0, keepdims=False) for item in (w_up, w_down)]
    )
    away_pair = lax.all_gather(away_pair, "hi", axis=0)
    away_got = lax.dynamic_index_in_dim(away_pair, away, 0, keepdims=False)
    up_got, down_got = away_got[0], away_got[1]
    up_own, down_own = (
        lax.dynamic_index_in_dim(item, 1 - away, 0, keepdims=False) for item in (w_up, w_down)
    )

    def from_experts(pieces):
        return [pieces[0]] + [permute_xor(pieces[j], "dp", j) for j in range(1, low)]

    o_all, qkv, xn1, w_mine, lse, slab, gain_first = call(
        functools.partial(attn_fwd_kernel, (half, dp, hpd, block, gain_lane, scale)),
        [
            ((length, width_h), BF16),
            ((length, cols), BF16),
            ((length, width), BF16),
            ((width, cols), BF16),
            ((length, LANES), F32),
            ((hpd, block, length), F32),
            ((1, width), F32),
        ],
        [meta] + own + sib + w_parts + [bias_rev],
        smem=1,
        name="attn_fwd",
        after=[cot_send, hot_rev],
    )
    o_mine = swap_seq(o_all.reshape(seq, rows, width_h))
    x1, xn2, probs, gain_second, send = call(
        functools.partial(mid_kernel, (seqs, groups, cp, slots, per_expert, experts)),
        [
            ((total, width), F32),
            ((total, width), BF16),
            ((total, experts), F32),
            ((1, width), F32),
        ]
        + [((2 * per_expert, width), BF16)],
        [o_mine, x_flat.reshape(total, width), ids_flat, slot_cols, w_small],
        name="mid",
        after=cot_parts[0],
    )

    slot_parts = to_experts(send)
    dx_sent, saved = [[], []], []
    for i in range(2):
        for j in range(low):
            dx_part, *rest = call(
                functools.partial(expert_kernel, (1, cp, slots)),
                [((per_expert, width), BF16)]
                + [((per_expert, ff), BF16)] * 4
                + [((per_expert, width), BF16)],
                [slot_parts[i][j], cot_parts[i][j], up_own, down_own, up_got, down_got],
                name="expert",
            )
            dx_sent[i].append(dx_part)
            saved.append(rest)
    dx_sum = []
    for i in range(2):
        dx_sum += call(
            functools.partial(add_kernel, (cp, slots)),
            [((per_expert, width), BF16)],
            from_experts(dx_sent[i]),
            name="add_dx",
        )
    y_sent = call(
        functools.partial(expert_out_kernel, (2 * low, 1)),
        [((per_expert, width), BF16)] * (2 * low),
        [item for one in saved for item in one[:2]] + [down_own, down_got],
        name="expert_out",
        after=[dx_sum[1]],
    )
    dx_swapped = permute_xor(dx_sum[1], "dp", low)
    grad_down, grad_down_away = call(
        functools.partial(down_grad_kernel, 2 * low),
        [((width, ff), F32), ((width, ff), BF16)],
        [item for one in saved for item in (one[0], one[1], one[4])],
        name="down_grad",
        after=[y_sent[0]],
    )
    grad_down_pair = lax.all_gather(grad_down_away, "hi", axis=0)
    ret_dx = [
        swap_seq(item.reshape(seq, cp, width)).reshape(per_expert, width)
        for item in (dx_sum[0], dx_swapped)
    ]
    y_back = [from_experts(y_sent[:low]), from_experts(y_sent[low:])]

    dx1, da, do_send, dlogits, prod = call(
        functools.partial(back_kernel, (seqs, groups, cp, slots, per_expert, local)),
        [
            ((total, width), F32),
            ((total, width), BF16),
            ((seq, rows, width_h), BF16),
            ((total, experts), F32),
            ((total, width), BF16),
        ],
        ret_dx
        + [x1, probs, ids_flat, slot_cols, cot_flat, w_small, gain_second],
        name="back",
        after=[y_sent[0], grad_down_away],
    )
    do_all = swap_seq(do_send).reshape(length, width_h)

    small_sent = call(
        functools.partial(small_grad_kernel, (seqs, groups)),
        [((width // dp, small_cols), BF16)] * dp,
        [meta, o_mine, da, xn2, dlogits, prod],
        scratch=[pltpu.VMEM((width, small_cols), BF16)],
        smem=1,
        name="small_grad",
    )
    small_got = [permute_xor(small_sent[j], "dp", j) if j else small_sent[j] for j in range(dp)]
    y_first, y_second = call(
        functools.partial(add_both_kernel, None),
        [((per_expert, width), BF16)] * 2,
        y_back[0] + y_back[1],
        name="add_y",
        after=[small_sent[0]],
    )

    y_swapped = permute_xor(y_second, "dp", low)
    (grad_up_away,) = call(
        functools.partial(up_grad_kernel, (2 * low, 1)),
        [((width, ff), BF16)],
        sum(slot_parts, []) + [one[3] for one in saved],
        name="up_grad_away",
        after=[y_swapped],
    )
    grad_up_pair = lax.all_gather(grad_up_away, "hi", axis=0)
    (y_pair,) = call(
        functools.partial(side_kernel, None),
        [((seq, 2 * cp, width), BF16)],
        [item.reshape(seq, cp, width) for item in (y_first, y_swapped)],
        name="side",
    )
    y_got = swap_seq(y_pair).reshape(seq, 2, cp, width)
    mixed_in = [y_got[:, k].reshape(per_expert, width) for k in range(2)]
    (mixed,) = call(
        functools.partial(mixed_kernel, (per_expert, local)),
        [((total, width), BF16)],
        mixed_in + [x1, probs, ids_flat, slot_cols],
        name="mixed",
    )


    span = length + block
    dx_own, dx_sib, dqkv, table_own = call(
        functools.partial(attn_bwd_kernel, (half, hpd, block, scale, rel_bias.shape[0])),
        [
            ((half, rows, width), BF16),
            ((half, rows, width), BF16),
            ((length, cols), BF16),
            ((8, LANES), F32),
        ],
        [meta, do_all, qkv, w_mine, lse, slab, hot_rev],
        scratch=[
            pltpu.VMEM((length, HD), F32),
            pltpu.VMEM((length, HD), F32),
            pltpu.VMEM((block, span), F32),
            pltpu.VMEM((8, span), F32),
        ],
        smem=1,
        name="attn_bwd",
        after=[y_pair, grad_up_away, small_sent[0]],
    )
    pairs = call(
        functools.partial(pair_kernel, None),
        [((rows, width), BF16)] * half,
        [dx_own, permute_xor(dx_sib, "seq", 1)],
        name="pair",
    )
    dx_parts = [permute_xor(pairs[k], "seq", 2 * k) if k else pairs[k] for k in range(half)]
    (grad_tokens,) = call(
        functools.partial(last_kernel, (half, seqs, groups)),
        [((total, width), BF16)],
        [meta] + dx_parts + [x_flat.reshape(total, width), dx1, gain_first],
        scratch=[pltpu.VMEM((seqs, rows, width), F32)],
        smem=1,
        name="last",
    )

    (grad_up,) = call(
        functools.partial(up_grad_kernel, (2 * low, 1)),
        [((width, ff), F32)],
        sum(slot_parts, []) + [one[2] for one in saved],
        name="up_grad",
        after=[pairs[0]],
    )
    cols_sent = call(
        functools.partial(cols_kernel, None),
        [((width // dp + 16, cols), BF16)] * dp,
        [meta, xn1, dqkv, table_own],
        scratch=[pltpu.VMEM((width, cols), BF16)],
        smem=1,
        name="cols",
        after=[pairs[0]],
    )
    cols_got = [permute_xor(cols_sent[j], "dp", j) if j else cols_sent[j] for j in range(dp)]
    line_rows = -(-shard // 8) * 8 + 8
    (line,) = call(
        functools.partial(merge_kernel, (dp, shard)),
        [((seq, line_rows, cols + small_cols), BF16)],
        cols_got + small_got,
        scratch=[pltpu.VMEM((width // dp, cols + small_cols), F32)],
        name="merge",
        after=dx_parts[1:] + [grad_up],
    )
    both_up, both_down = call(
        functools.partial(both_experts_kernel, None),
        [((local, width, ff), F32)] * 2,
        [meta, grad_up, grad_up_pair, grad_down, grad_down_pair],
        smem=1,
        name="both_experts",
    )
    grad_qkv, grad_out, grad_router, grad_first, grad_second, table = call(
        functools.partial(finish_kernel, (seqs, groups, hpd, cols, experts)),
        [
            ((shard, 3 * width), F32),
            ((shard, width), F32),
            ((shard, experts), F32),
            ((1, shard), F32),
            ((1, shard), F32),
            ((8, LANES), F32),
        ],
        [swap_seq(line), w_qkv, gain_attn[:, None]],
        name="finish",
        after=[grad_tokens, mixed, both_up],
    )
    table = table.reshape(8, repeat, rel_bias.shape[0])
    table = jnp.transpose(table, (2, 1, 0)).reshape(rel_bias.shape[0], 8 * repeat)
    table_grad = table[:, :heads]

    return (
        mixed.reshape(tokens.shape),
        grad_tokens.reshape(tokens.shape),
        grad_first.reshape(shard),
        grad_qkv,
        table_grad,
        grad_out,
        grad_second.reshape(shard),
        grad_router,
        both_up,
        both_down,
    )


def solution(mesh):
    dp, seq = mesh.devices.shape
    mesh = Mesh(mesh.devices.reshape(2, dp // 2, seq), DP + ("seq",))
    in_specs = (
        P(None, DP, "seq", None),
        P(None, DP, "seq", None),
        P(None, DP, "seq", None),
        P(),
        P(("hi", "lo", "seq")),
        P(("hi", "lo", "seq"), None),
        P(),
        P(("hi", "lo", "seq"), None),
        P(("hi", "lo", "seq")),
        P(("hi", "lo", "seq"), None),
        P("seq", None, DP),
        P("seq", None, DP),
    )
    out_specs = (
        P(None, DP, "seq", None),
        P(None, DP, "seq", None),
        P(("hi", "lo", "seq")),
        P(("hi", "lo", "seq"), None),
        P(),
        P(("hi", "lo", "seq"), None),
        P(("hi", "lo", "seq")),
        P(("hi", "lo", "seq"), None),
        P("seq", None, DP),
        P("seq", None, DP),
    )
    return jax.shard_map(shards, mesh=mesh, in_specs=in_specs, out_specs=out_specs, check_vma=False)
```
